256 devices in a mesh: batch: 8 (over x, core), seq: 32 (over y, z).
Axes of the slice: x: 4, y: 4, z: 8, core: 2. Of those that a mesh axis runs over, the one named last changes fastest.
Arguments:
- behaviors: bfloat16 [8, 8192, 1024], P('batch', 'seq'), may hold values from -100 to 100
- log_decay: float32 [8, 8, 8192], P('batch', None, 'seq'), may hold values from -1 to 0
- qkv_weight: bfloat16 [1024, 3072], replicated, may hold values from -0.1875 to 0.1875
- cotangent: bfloat16 [8, 8192, 1024], P('batch', 'seq'), may hold values from -6 to 6
Outputs:
- mixed: bfloat16 [8, 8192, 1024], P('batch', 'seq')
- d_behaviors: bfloat16 [8, 8192, 1024], P('batch', 'seq')
- weight_step: float32 [1024, 3072], P('seq')
The draws below stay inside these ranges and needn't reach their ends.
All inputs are finite; a program needn't handle non-finite values.
Results may differ from the reference program's by a relative error of at most 0.0095.
Values sent between devices are 32-bit elements; how exact they have to be, the bound alone decides.
No kernel may reach another device: no remote copies, remote signals or barrier semaphores. Data moves between devices by JAX's collectives and lax.ppermute only.
A program may use at most 128 MiB of HBM per device.

```python
import math
import jax
import jax.numpy as jnp
from jax import lax

HEAD_COUNT = 8
HD = 128
D = 1024
TOK_DEV = 256
HISTORY_TOKENS = 8192
USER_COUNT = 8


def draw_behaviors(key, part):
    key = jax.random.fold_in(key, 3)
    noise_key, column_key = jax.random.split(key, 2)
    columns = jnp.arange(D, dtype=jnp.float32) / D
    column_scale = jnp.exp(math.log(10.0) * columns + jax.random.uniform(column_key, (D,), jnp.float32, -0.35, 0.35))
    noise_draw = jnp.clip(jax.random.normal(noise_key, (USER_COUNT, HISTORY_TOKENS, D), jnp.float32), -4.0, 4.0)
    return (noise_draw * column_scale).astype(jnp.bfloat16)


def draw_log_decay(key, part):
    key = jax.random.fold_in(key, 5)
    every_key_row = jax.random.split(key, 7)
    slow_share = 0.5
    blocks = HISTORY_TOKENS // TOK_DEV
    slow_heads = jax.random.uniform(every_key_row[0], (USER_COUNT, HEAD_COUNT, 1), jnp.float32) < slow_share
    slow_rate = jax.random.uniform(every_key_row[1], (USER_COUNT, HEAD_COUNT, 1), jnp.float32, 0.05, 0.3) / HISTORY_TOKENS
    fast_rate = jax.random.uniform(every_key_row[2], (USER_COUNT, HEAD_COUNT, 1), jnp.float32, 1.0 / 50.0, 1.0 / 30.0)
    decay_rate_floor = jnp.where(slow_heads, slow_rate, fast_rate)
    partition_factor = jnp.exp(jax.random.uniform(every_key_row[3], (USER_COUNT, HEAD_COUNT, blocks), jnp.float32, math.log(0.5), math.log(2.0)))
    partition_factor = jnp.repeat(partition_factor, TOK_DEV, axis=2)
    jagged_amount = jax.random.uniform(every_key_row[4], (USER_COUNT, HEAD_COUNT, HISTORY_TOKENS), jnp.float32, 0.5, 1.5)
    spike_positions = jax.random.randint(every_key_row[5], (USER_COUNT, HEAD_COUNT, 2), 0, HISTORY_TOKENS)
    spike_penalty = jax.random.uniform(every_key_row[6], (USER_COUNT, HEAD_COUNT, 2), jnp.float32, 0.2, 0.4)
    token_places = jnp.arange(HISTORY_TOKENS)[None, None, None, :]
    match_count = token_places == spike_positions[:, :, :, None]
    spike_events = jnp.sum(jnp.where(match_count, jnp.log(1.0 - spike_penalty)[:, :, :, None], 0.0), axis=2)
    return -decay_rate_floor * partition_factor * jagged_amount + spike_events


def block_levels(key, dims, cuts, smallest, largest):
    loudness, own = 1.0, jax.random.fold_in(key, 6)
    for axis_at, blocks in cuts:
        heights = jnp.exp(jax.random.uniform(jax.random.fold_in(own, axis_at), (blocks,), jnp.float32, smallest / len(cuts), largest / len(cuts)))
        loudness = loudness * jnp.repeat(heights, dims[axis_at] // blocks).reshape([-1 if axis == axis_at else 1 for axis in range(len(dims))])
    return loudness


def centred(stream_key, shape, width, reach, shards=(), kind=jnp.bfloat16):
    drawn = jax.random.normal(stream_key, shape, jnp.float32) * width
    if len(shards) > 0:
        drawn = block_levels(stream_key, shape, shards, -0.22, 0.18) * drawn
    return jnp.clip(drawn, min=-reach, max=reach).astype(kind)


def setup_inputs(seed: int = 0) -> dict:
    streams_of = jax.random.split(jax.random.key(seed), 5)
    return {
        "behaviors": draw_behaviors(jax.random.fold_in(streams_of[4], 71), 0),
        "log_decay": draw_log_decay(jax.random.fold_in(streams_of[4], 71), 0),
        "qkv_weight": centred(streams_of[2], (D, 3 * D), D ** -0.5, 0.1875),
        "cotangent": centred(streams_of[3], (USER_COUNT, HISTORY_TOKENS, D), 1.0, 6.0, ((0, 8), (1, 32))),
    }


epsilon = 1e-06

def split_heads(packed):
    length = packed.shape[0]
    pieces = packed.reshape(length, 3, HEAD_COUNT, HD)
    return (pieces[:, 0], pieces[:, 1], pieces[:, 2])

def decay_tables(log_rates):
    cumulative = jnp.cumsum(log_rates, axis=1)
    length = log_rates.shape[1]
    causal = (jnp.arange(length)[:, None] >= jnp.arange(length)[None, :])[None]
    spread = cumulative[:, :, None] - cumulative[:, None, :]
    within = jnp.where(causal, jnp.exp(jnp.where(causal, spread, 0.0)), 0.0)
    last_log = cumulative[:, -1]
    entering = jnp.exp(cumulative)
    leaving = jnp.exp(last_log[:, None] - cumulative)
    return (within, entering, leaving, jnp.exp(last_log))

def forward_block(rows, log_rates, weight, state_in):
    flt = jnp.float32
    packed = jnp.dot(rows, weight, preferred_element_type=flt).astype(jnp.bfloat16)
    queries, key_rows, values = split_heads(packed)
    within, entering, leaving, carry_rate = decay_tables(log_rates)
    scores = jnp.einsum('thd,shd->hts', queries.astype(flt), key_rows.astype(flt))
    weights_bf = (scores * within).astype(jnp.bfloat16)
    intra = jnp.einsum('hts,she->the', weights_bf.astype(flt), values.astype(flt))
    state_bf = state_in.astype(jnp.bfloat16)
    inter = jnp.einsum('thd,hde->the', queries.astype(flt), state_bf.astype(flt)) * entering.T[:, :, None]
    output = intra + inter
    scale = lax.rsqrt(lax.optimization_barrier(jnp.mean(output * output, axis=-1, keepdims=True)) + epsilon)
    normed = output * scale
    keyed = (key_rows.astype(flt) * leaving.T[:, :, None]).astype(jnp.bfloat16)
    local_sum = jnp.einsum('thd,the->hde', keyed.astype(flt), values.astype(flt))
    state_out = carry_rate[:, None, None] * state_in + local_sum
    return (packed, weights_bf, within, entering, leaving, carry_rate, normed, scale, state_bf, state_out)

def backward_block(rows, log_rates, weight, state_in, grad_next, upstream):
    flt = jnp.float32
    saved = forward_block(rows, log_rates, weight, state_in)
    packed, weights_bf, within, entering, leaving, carry_rate, normed, scale, state_bf, state_out = saved
    queries, key_rows, values = split_heads(packed)
    length = rows.shape[0]
    incoming = upstream.astype(flt).reshape(length, HEAD_COUNT, HD)
    d_output = (scale * (incoming - normed * lax.optimization_barrier(jnp.mean(normed * incoming, axis=-1, keepdims=True)))).astype(jnp.bfloat16)
    d_prob = jnp.einsum('the,she->hts', d_output.astype(flt), values.astype(flt))
    d_score = (d_prob * within).astype(jnp.bfloat16)
    back_bf = grad_next.astype(jnp.bfloat16)
    d_query = jnp.einsum('hts,shd->thd', d_score.astype(flt), key_rows.astype(flt))
    d_query = d_query + entering.T[:, :, None] * jnp.einsum('the,hde->thd', d_output.astype(flt), state_bf.astype(flt))
    d_key = jnp.einsum('hts,thd->shd', d_score.astype(flt), queries.astype(flt))
    d_key = d_key + leaving.T[:, :, None] * jnp.einsum('the,hde->thd', values.astype(flt), back_bf.astype(flt))
    d_value = jnp.einsum('hts,the->she', weights_bf.astype(flt), d_output.astype(flt))
    d_value = d_value + leaving.T[:, :, None] * jnp.einsum('thd,hde->the', key_rows.astype(flt), back_bf.astype(flt))
    lifted = (queries.astype(flt) * entering.T[:, :, None]).astype(jnp.bfloat16)
    collected = jnp.einsum('thd,the->hde', lifted.astype(flt), d_output.astype(flt))
    grad_here = collected + carry_rate[:, None, None] * grad_next
    d_packed = jnp.stack([d_query, d_key, d_value], axis=1).reshape(length, 3 * D).astype(jnp.bfloat16)
    d_rows = jnp.dot(d_packed, weight.T, preferred_element_type=flt).astype(jnp.bfloat16)
    term = jnp.dot(rows.T, d_packed, preferred_element_type=flt)
    return (grad_here, d_rows, term)

def reference(behaviors, log_decay, qkv_weight, cotangent):
    blocks = HISTORY_TOKENS // TOK_DEV

    def one_user(grad_total, inputs):
        rows_all, rates_all, upstream_all = inputs
        row_blocks = rows_all.reshape(blocks, TOK_DEV, D)
        rate_blocks = rates_all.reshape(HEAD_COUNT, blocks, TOK_DEV).transpose(1, 0, 2)
        up_blocks = upstream_all.reshape(blocks, TOK_DEV, D)

        def forward_step(state, pieces):
            rows, rates = pieces
            result = forward_block(rows, rates, qkv_weight, state)
            return (result[-1], (result[6].reshape(TOK_DEV, D).astype(jnp.bfloat16), state))
        zero_state = jnp.zeros((HEAD_COUNT, HD, HD), jnp.float32)
        final_state, (outputs, entering_states) = lax.scan(forward_step, zero_state, (row_blocks, rate_blocks))

        def backward_step(carry, pieces):
            grad_next, grad_sum = carry
            rows, rates, state_in, upstream = pieces
            grad_here, d_rows, term = backward_block(rows, rates, qkv_weight, state_in, grad_next, upstream)
            return ((grad_here, grad_sum + term), d_rows)
        (first_grad, grad_total), d_blocks = lax.scan(backward_step, (zero_state, grad_total), (row_blocks, rate_blocks, entering_states, up_blocks), reverse=True)
        return (grad_total, (outputs.reshape(HISTORY_TOKENS, D), d_blocks.reshape(HISTORY_TOKENS, D)))
    grad_zero = jnp.zeros((D, 3 * D), jnp.float32)
    grad_total, (mixed, d_behaviors) = lax.scan(one_user, grad_zero, (behaviors, log_decay, cotangent))
    grouped = grad_total.reshape(D, 3, D)
    square_mean = lax.optimization_barrier(jnp.mean(grouped * grouped, axis=(0, 2)))
    weight_step = (grouped * lax.rsqrt(square_mean + epsilon)[None, :, None]).reshape(D, 3 * D)
    return (mixed, d_behaviors, weight_step)
```

```python
import functools

import jax
import jax.numpy as jnp
from jax import lax
from jax.experimental import pallas as pl
from jax.experimental.pallas import tpu as pltpu
from jax.sharding import PartitionSpec as P

epsilon = 1e-06
flt = jnp.float32
half = jnp.bfloat16
PAIR = 2
CORES = 2
EXTRA = 8


def dot(a, b, ca, cb, precision=None):
    return lax.dot_general(
        a, b, (((ca,), (cb,)), ((), ())), preferred_element_type=flt, precision=precision
    )


def ordered(length):
    at = lax.broadcasted_iota(jnp.int32, (length, length), 0)
    source = lax.broadcasted_iota(jnp.int32, (length, length), 1)
    return at >= source


def running(rates):
    ones = ordered(rates.shape[1]).astype(flt)
    exact = lax.Precision.HIGHEST
    return dot(ones, rates, 1, 1, exact), dot(rates, ones, 1, 1, exact)


def decay_within(tall, flat, index):
    length = tall.shape[0]
    causal = ordered(length)
    spread = tall[:, index : index + 1] - flat[index : index + 1, :]
    return jnp.where(causal, jnp.exp(jnp.where(causal, spread, 0.0)), 0.0)


def place_in(index, step, count):
    return lax.rem(index + step + count, count)


def project_kernel(size, at_ref, rows_ref, wq_ref, wk_ref, wv_ref, rates_ref, *refs):
    q_ref, k_ref, v_ref, tall_ref, flat_ref = refs[:5]
    sent_refs, (slots_ref, leaving_ref) = refs[5:-2], refs[-2:]
    heads = len(sent_refs)
    line = lax.rem(at_ref[1], heads)
    step = pl.program_id(0)
    rows = rows_ref[...]

    @pl.when(step == 0)
    def _():
        tall, flat = running(rates_ref[...])
        tall_ref[...] = tall
        flat_ref[...] = flat
        leaving_ref[...] = jnp.exp(tall[-1:] - tall)

    k = dot(rows, wk_ref[...], 1, 0).astype(half)
    v = dot(rows, wv_ref[...], 1, 0).astype(half)
    k_ref[...] = k
    v_ref[...] = v
    leaving = leaving_ref[...]
    lanes = lax.broadcasted_iota(jnp.int32, leaving.shape, 1)
    for lane in range(PAIR):
        at = slice(lane * size, (lane + 1) * size)
        head = step * PAIR + lane
        column = jnp.sum(jnp.where(lanes == head, leaving, 0.0), axis=1, keepdims=True)
        keyed = (k[:, at].astype(flt) * column).astype(half)
        slot = place_in(head, -line, heads)
        slots_ref[slot, :size, :] = dot(keyed, v[:, at], 0, 0)
        last = flat_ref[pl.ds(head, 1), :][:, -1:]
        slots_ref[slot, size:, :] = jnp.broadcast_to(jnp.exp(last), (EXTRA, size))
    q_ref[...] = dot(rows, wq_ref[...], 1, 0).astype(half)

    @pl.when(step == pl.num_programs(0) - 1)
    def _():
        for slot, sent_ref in enumerate(sent_refs):
            sent_ref[...] = slots_ref[slot]


def line_kernel(at_ref, *refs):
    got_refs, (sums_ref, rates_ref, total_ref) = refs[:-3], refs[-3:]
    blocks = len(got_refs)
    line = lax.rem(at_ref[1], blocks)
    size = total_ref.shape[1]
    for step, got_ref in enumerate(got_refs):
        block = place_in(line, -step, blocks)
        sums_ref[block] = got_ref[:size, :]
        rates_ref[block] = got_ref[size:, :]
    state = jnp.zeros((size, size), flt)
    rate = jnp.ones((EXTRA, size), flt)
    for block in range(blocks):
        state = rates_ref[block, :1, :] * state + sums_ref[block]
        rate = rate * rates_ref[block]
    total_ref[:size, :] = state
    total_ref[size:, :] = rate


def spread_kernel(at_ref, sums_ref, rates_ref, *refs):
    blocks = sums_ref.shape[0]
    size = sums_ref.shape[1]
    out_refs, keep_ref, totals_ref, states_ref = refs[-blocks - 3 : -3], refs[-3], refs[-2], refs[-1]
    got_refs = refs[: -blocks - 3]
    segments = len(got_refs)
    line = lax.rem(at_ref[1], blocks)
    mine = at_ref[1] // blocks
    for step, got_ref in enumerate(got_refs):
        totals_ref[place_in(mine, -step, segments)] = got_ref[...]
    state = jnp.zeros((size, size), flt)
    for segment in range(segments):
        after = totals_ref[segment, size : size + 1, :] * state + totals_ref[segment, :size, :]
        state = jnp.where(segment < mine, after, state)
        keep_ref[segment] = totals_ref[segment, size:, :]
    for block in range(blocks):
        states_ref[block] = state
        state = rates_ref[block, :1, :] * state + sums_ref[block]
    for step, out_ref in enumerate(out_refs):
        out_ref[...] = states_ref[place_in(line, step, blocks)]


def back_line_kernel(at_ref, rates_ref, *refs):
    got_refs, (sums_ref, total_ref) = refs[:-2], refs[-2:]
    blocks = len(got_refs)
    line = lax.rem(at_ref[1], blocks)
    for step, got_ref in enumerate(got_refs):
        sums_ref[place_in(line, -step, blocks)] = got_ref[...]
    state = jnp.zeros(total_ref.shape, flt)
    for block in range(blocks - 1, -1, -1):
        state = rates_ref[block, :1, :] * state + sums_ref[block]
    total_ref[...] = state


def back_spread_kernel(at_ref, sums_ref, rates_ref, keep_ref, *refs):
    blocks = sums_ref.shape[0]
    size = sums_ref.shape[1]
    out_refs, totals_ref, states_ref = refs[-blocks - 2 : -2], refs[-2], refs[-1]
    got_refs = refs[: -blocks - 2]
    segments = len(got_refs)
    line = lax.rem(at_ref[1], blocks)
    mine = at_ref[1] // blocks
    for step, got_ref in enumerate(got_refs):
        totals_ref[place_in(mine, -step, segments)] = got_ref[...]
    state = jnp.zeros((size, size), flt)
    for segment in range(segments - 1, -1, -1):
        after = keep_ref[segment, :1, :] * state + totals_ref[segment]
        state = jnp.where(segment > mine, after, state)
    for block in range(blocks - 1, -1, -1):
        states_ref[block] = state
        state = rates_ref[block, :1, :] * state + sums_ref[block]
    for step, out_ref in enumerate(out_refs):
        out_ref[...] = states_ref[place_in(line, step, blocks)]


def weights_kernel(heads, size, q_ref, k_ref, v_ref, tall_ref, flat_ref, weights_ref, intra_ref):
    tall, flat = tall_ref[...], flat_ref[...]
    for head in range(heads):
        at = slice(head * size, (head + 1) * size)
        scores = dot(q_ref[:, at], k_ref[:, at], 1, 1)
        weights = (scores * decay_within(tall, flat, head)).astype(half)
        weights_ref[head] = weights
        intra_ref[:, at] = dot(weights, v_ref[:, at], 1, 0)


def mix_kernel(size, at_ref, q_ref, intra_ref, up_ref, tall_ref, *refs):
    heads = (len(refs) - 4) // 2
    state_refs, mixed_ref, dout_ref, keep_ref = refs[:heads], refs[heads], refs[heads + 1], refs[heads + 2]
    sent_refs, slots_ref = refs[heads + 3 : -1], refs[-1]
    line = lax.rem(at_ref[1], heads)
    entering = jnp.exp(tall_ref[...])
    for step, state_ref in enumerate(state_refs):
        keep_ref[place_in(line, -step, heads)] = state_ref[...]
    for head in range(heads):
        at = slice(head * size, (head + 1) * size)
        q = q_ref[:, at]
        column = entering[:, head : head + 1]
        output = intra_ref[:, at] + dot(q, keep_ref[head].astype(half), 1, 0) * column
        scale = lax.rsqrt(jnp.mean(output * output, axis=-1, keepdims=True) + epsilon)
        normed = output * scale
        mixed_ref[:, at] = normed.astype(half)
        incoming = up_ref[:, at].astype(flt)
        along = jnp.mean(normed * incoming, axis=-1, keepdims=True)
        d_output = (scale * (incoming - normed * along)).astype(half)
        dout_ref[:, at] = d_output
        lifted = (q.astype(flt) * column).astype(half)
        slots_ref[place_in(head, -line, heads)] = dot(lifted, d_output, 0, 0)
    for slot, sent_ref in enumerate(sent_refs):
        sent_ref[...] = slots_ref[slot]


def copies_kernel(rows_ref, out_ref):
    wide = rows_ref[...].astype(flt)
    for copy in range(out_ref.shape[0]):
        out_ref[copy] = wide


def pack_kernel(size, dout_ref, state_ref, rates_ref, out_ref):
    length = dout_ref.shape[0]
    for head in range(out_ref.shape[0]):
        out_ref[head, :length, :] = dout_ref[:, head * size : (head + 1) * size].astype(flt)
        out_ref[head, length : length + size, :] = state_ref[head]
        row = rates_ref[head : head + 1, :]
        out_ref[head, length + size :, :] = jnp.zeros((EXTRA, size), flt)
        for part in range(length // size):
            place = length + size + part
            out_ref[head, place : place + 1, :] = row[:, part * size : (part + 1) * size]


def recall_kernel(at_ref, mine_ref, other_ref, wq_ref, wk_ref, wv_ref, rows_ref, qkv_ref):
    core = lax.rem(at_ref[0], CORES)
    weight = jnp.concatenate([wq_ref[...], wk_ref[...], wv_ref[...]], axis=1)
    for slot, wide_ref in ((core, mine_ref), (1 - core, other_ref)):
        rows = wide_ref[0].astype(half)
        rows_ref[slot] = rows
        qkv_ref[slot] = dot(rows, weight, 1, 0).astype(half)


def inner_grads(q, k, v, d_output, weights, state, within, entering):
    d_score = (dot(d_output, v, 1, 1) * within).astype(half)
    d_query = dot(d_score, k, 1, 0) + entering * dot(d_output, state, 1, 1)
    return d_query.astype(half), dot(d_score, q, 0, 0), dot(weights, d_output, 0, 0)


def owner_kernel(size, qkv_ref, got_ref, tall_ref, turned_ref, dk_ref, dv_ref):
    users, length, _ = qkv_ref.shape
    rates = jnp.concatenate(
        [
            jnp.concatenate(
                [got_ref[user, length + size + part : length + size + part + 1, :] for part in range(length // size)],
                axis=1,
            )
            for user in range(users)
        ],
        axis=0,
    )
    tall, flat = running(rates)
    tall_ref[...] = tall
    entering = jnp.exp(tall)
    for user in range(users):
        q, k, v = (qkv_ref[user, :, part * size : (part + 1) * size] for part in range(3))
        within = decay_within(tall, flat, user)
        weights = (dot(q, k, 1, 1) * within).astype(half)
        d_output = got_ref[user, :length, :].astype(half)
        state = got_ref[user, length : length + size, :].astype(half)
        d_query, dk_ref[user], dv_ref[user] = inner_grads(
            q, k, v, d_output, weights, state, within, entering[:, user : user + 1]
        )
        turned_ref[:, user * length : (user + 1) * length] = d_query.T


def late_kernel(size, at_ref, qkv_ref, dk_ref, dv_ref, tall_ref, *refs):
    users, length, _ = qkv_ref.shape
    back_refs, (out_ref, slots_ref) = refs[:users], refs[users:]
    chips = users // CORES
    chip, core = at_ref[0] // CORES, lax.rem(at_ref[0], CORES)
    for place, back_ref in enumerate(back_refs):
        step, turn = place // CORES, place % CORES
        user = place_in(chip, -step, chips) * CORES + lax.rem(core + turn, CORES)
        slots_ref[user] = back_ref[...].astype(half)
    tall = tall_ref[...]
    leaving = jnp.exp(tall[-1:] - tall)
    for user in range(users):
        at = slice(user * length, (user + 1) * length)
        column = leaving[:, user : user + 1]
        k = qkv_ref[user, :, size : 2 * size]
        v = qkv_ref[user, :, 2 * size :]
        back = slots_ref[user]
        d_key = (dk_ref[user] + column * dot(v, back, 1, 1)).astype(half)
        d_value = (dv_ref[user] + column * dot(k, back, 1, 0)).astype(half)
        out_ref[:size, at] = d_key.T
        out_ref[size:, at] = d_value.T


def choose_kernel(size, at_ref, *refs):
    heads = (len(refs) - 2) // 2
    back_refs, out_refs, keep_ref, slots_ref = refs[:heads], refs[heads:-2], refs[-2], refs[-1]
    chips = heads // CORES
    line = lax.rem(at_ref[1], heads)
    chip, core = at_ref[0] // CORES, lax.rem(at_ref[0], CORES)
    for step, back_ref in enumerate(back_refs):
        slots_ref[place_in(line, -step, heads)] = back_ref[...]
    for place, out_ref in enumerate(out_refs):
        step, turn = place // CORES, place % CORES
        out_ref[...] = slots_ref[place_in(chip, step, chips) * CORES + lax.rem(core + turn, CORES)]
    keep_ref[...] = slots_ref[...].astype(half)


def term_kernel(size, step, segments, at_ref, dq_ref, dkv_ref, rows_ref, out_ref):
    users, length, width = rows_ref.shape
    heads = width // size
    share = width // segments
    target = place_in(at_ref[1] // heads, step, segments)
    columns = rows_ref[:, :, pl.ds(pl.multiple_of(target * share, share), share)]
    columns = columns.reshape(users * length, share)
    out_ref[:size, :] = dot(dq_ref[...], columns, 1, 0)
    out_ref[size:, :] = dot(dkv_ref[...], columns, 1, 0)


def fold_kernel(at_ref, *refs):
    blocks = len(refs) - 5
    got_refs, out_refs, slots_ref = refs[:4], refs[4:-1], refs[-1]
    total = got_refs[0][...]
    for got_ref in got_refs[1:]:
        total += got_ref[...]
    turned = total.T
    line = lax.rem(at_ref[1], blocks)
    share = turned.shape[0] // blocks
    for block in range(blocks):
        slots_ref[block] = turned[block * share : (block + 1) * share]
    for step, out_ref in enumerate(out_refs):
        out_ref[...] = slots_ref[place_in(line, step, blocks)]


def gather_kernel(*refs):
    total = refs[0][...]
    for got_ref in refs[1:-1]:
        total += got_ref[...]
    refs[-1][...] = total


def both_kernel(mine_ref, other_ref, out_ref):
    out_ref[0] = mine_ref[...]
    out_ref[1] = other_ref[...]


def square_kernel(*refs):
    got_refs, out_ref = refs[:-1], refs[-1]
    size = out_ref.shape[2]
    for part in range(3):
        total = jnp.zeros((1, size), flt)
        for got_ref in got_refs:
            for core in range(CORES):
                piece = got_ref[core, :, part * size : (part + 1) * size]
                total += jnp.sum(piece * piece, axis=0, keepdims=True)
        out_ref[:, part : part + 1, :] = jnp.broadcast_to(total[None], (out_ref.shape[0], 1, size))
    out_ref[:, 3:, :] = jnp.zeros((out_ref.shape[0], EXTRA - 3, size), flt)


def step_kernel(at_ref, squares_ref, *refs):
    got_refs, out_ref, slots_ref = refs[:-2], refs[-2], refs[-1]
    heads, share, width = slots_ref.shape
    size = width // 3
    chips = heads // CORES
    chip, core = at_ref[0] // CORES, lax.rem(at_ref[0], CORES)
    for step, got_ref in enumerate(got_refs):
        for turn in range(CORES):
            head = place_in(chip, -step, chips) * CORES + lax.rem(core + turn, CORES)
            slots_ref[head] = got_ref[turn]
    total = jnp.sum(squares_ref[...], axis=0)
    entries = float(heads * size) ** 2
    for part in range(3):
        mean = jnp.sum(total[part : part + 1], axis=1, keepdims=True) / entries
        factor = lax.rsqrt(mean + epsilon)
        for head in range(heads):
            at = (part * heads + head) * size
            out_ref[:, at : at + size] = slots_ref[head, :, part * size : (part + 1) * size] * factor


def rows_kernel(size, dq_ref, dki_ref, dvi_ref, k_ref, v_ref, back_ref, tall_ref,
                wq_ref, wk_ref, wv_ref, out_ref, dk_ref, dv_ref):
    @pl.when(pl.program_id(0) == 0)
    def _():
        tall = tall_ref[...]
        leaving = jnp.exp(tall[-1:] - tall)
        for head in range(back_ref.shape[0]):
            at = slice(head * size, (head + 1) * size)
            column = leaving[:, head : head + 1]
            back = back_ref[head]
            dk_ref[:, at] = (dki_ref[:, at] + column * dot(v_ref[:, at], back, 1, 1)).astype(half)
            dv_ref[:, at] = (dvi_ref[:, at] + column * dot(k_ref[:, at], back, 1, 0)).astype(half)

    total = dot(dq_ref[...], wq_ref[...], 1, 1)
    total += dot(dk_ref[...], wk_ref[...], 1, 1)
    total += dot(dv_ref[...], wv_ref[...], 1, 1)
    out_ref[...] = total.astype(half)


def inner_kernel(size, q_ref, k_ref, v_ref, dout_ref, weights_ref, state_ref, tall_ref, flat_ref,
                 dq_ref, dk_ref, dv_ref):
    tall, flat = tall_ref[...], flat_ref[...]
    entering = jnp.exp(tall)
    for head in range(weights_ref.shape[0]):
        at = slice(head * size, (head + 1) * size)
        dq_ref[:, at], dk_ref[:, at], dv_ref[:, at] = inner_grads(
            q_ref[:, at], k_ref[:, at], v_ref[:, at], dout_ref[:, at], weights_ref[head],
            state_ref[head].astype(half), decay_within(tall, flat, head), entering[:, head : head + 1]
        )


def shape(dims, kind=flt):
    return jax.ShapeDtypeStruct(dims, kind)


def kernel(body, out_shape, flops, moved, name, placed=True, limit=16, **more):
    cost = pl.CostEstimate(flops=int(flops), bytes_accessed=int(moved), transcendentals=0)
    settings = dict(
        out_shape=out_shape,
        compiler_params=pltpu.CompilerParams(vmem_limit_bytes=limit << 20),
        cost_estimate=cost,
        name=name,
    )
    settings.update(more)
    return lambda *arrays: pl.pallas_call(
        body,
        in_specs=[pl.BlockSpec(memory_space=pltpu.SMEM if placed and n == 0 else pltpu.VMEM) for n in range(len(arrays))],
        **settings,
    )(*arrays)


def on_device(behaviors, log_decay, qkv_weight, cotangent):
    rows = behaviors[0]
    rates = log_decay[0]
    upstream = cotangent[0]
    length, width = rows.shape
    heads = rates.shape[0]
    size = width // heads
    users = lax.axis_size("batch")
    count = lax.axis_size("seq")
    segments = count // heads
    chips = users // CORES
    pairs = heads // PAIR
    wide = PAIR * size
    at = jnp.stack([lax.axis_index("batch"), lax.axis_index("seq")]).astype(jnp.int32)

    def along_line(array, step):
        pairs_of = [(s, s // heads * heads + (s + step) % heads) for s in range(count)]
        return lax.ppermute(array, "seq", pairs_of)

    def along_segments(array, step):
        return lax.ppermute(array, "seq", [(s, (s + step * heads) % count) for s in range(count)])

    def along_users(array, step, turn):
        pairs_of = [
            (u, (u // CORES + step) % chips * CORES + (u + turn) % CORES) for u in range(users)
        ]
        return lax.ppermute(array, "batch", pairs_of)

    def line_exchange(arrays):
        return [arrays[0]] + [along_line(arrays[step], step) for step in range(1, heads)]

    def segment_exchange(array):
        return [array] + [along_segments(array, step) for step in range(1, segments)]

    whole = lambda dims: pl.BlockSpec(dims, lambda i: (0,) * len(dims))
    column = pl.BlockSpec((length, wide), lambda i: (0, i))
    weight_at = lambda part: pl.BlockSpec((width, wide), lambda i: (0, part * pairs + i))
    tokens = lambda kind: shape((length, width), kind)
    state = shape((size, size))
    states = shape((heads, size, size))
    carried = shape((size + EXTRA, size))
    smem = pl.BlockSpec(memory_space=pltpu.SMEM)
    square = length * length * size

    projected = pl.pallas_call(
        functools.partial(project_kernel, size),
        grid=(pairs,),
        in_specs=[smem, whole((length, width)), weight_at(0), weight_at(1), weight_at(2), whole((heads, length))],
        out_specs=[column] * 3 + [whole((length, heads)), whole((heads, length))]
        + [whole((size + EXTRA, size))] * heads,
        out_shape=[tokens(half)] * 3 + [shape((length, heads)), shape((heads, length))] + [carried] * heads,
        scratch_shapes=[pltpu.VMEM((heads, size + EXTRA, size), flt), pltpu.VMEM((length, heads), flt)],
        compiler_params=pltpu.CompilerParams(vmem_limit_bytes=16 << 20),
        cost_estimate=pl.CostEstimate(
            flops=6 * length * width * width, bytes_accessed=8 * width * width, transcendentals=0
        ),
        name="project",
    )(at, rows, qkv_weight, qkv_weight, qkv_weight, rates)
    q, k, v, tall, flat = projected[:5]

    got = line_exchange(projected[5:])
    sums, block_rates, total = kernel(
        line_kernel, [states, shape((heads, EXTRA, size)), carried], 1 << 20, 1 << 20, "line"
    )(at, *got)
    got = segment_exchange(total)
    spread = kernel(
        spread_kernel, [state] * heads + [shape((segments, EXTRA, size))], 1 << 20, 1 << 20, "spread",
        scratch_shapes=[
            pltpu.VMEM((segments, size + EXTRA, size), flt),
            pltpu.VMEM((heads, size, size), flt),
        ],
    )(at, sums, block_rates, *got)
    segment_rates = spread[-1]
    state_got = line_exchange(spread[:-1])

    copies = kernel(copies_kernel, shape((chips, length, width)), 1 << 20, 6 << 20, "copies", False)(rows)
    groups = [[chip * CORES + core for chip in range(chips)] for core in range(CORES)]
    rows_mine = lax.all_to_all(copies, "batch", 0, 0, axis_index_groups=groups)
    rows_other = along_users(rows_mine, 0, 1)

    weights, intra = kernel(
        functools.partial(weights_kernel, heads, size),
        [shape((heads, length, length), half), tokens(flt)],
        heads * 4 * square, 5 << 20, "weights", False,
    )(q, k, v, tall, flat)

    mixing = kernel(
        functools.partial(mix_kernel, size),
        [tokens(half), tokens(half), states] + [state] * heads,
        heads * 2 * square, 5 << 20, "mix",
        scratch_shapes=[pltpu.VMEM((heads, size, size), flt)],
    )(at, q, intra, upstream, tall, *state_got)
    mixed, d_output, state_in = mixing[:3]

    got = line_exchange(mixing[3:])
    back_sums, total = kernel(back_line_kernel, [states, state], 1 << 20, 1 << 20, "back_line")(
        at, block_rates, *got
    )
    got = segment_exchange(total)
    spread = kernel(
        back_spread_kernel, [state] * heads, 1 << 20, 1 << 20, "back_spread",
        scratch_shapes=[pltpu.VMEM((segments, size, size), flt), pltpu.VMEM((heads, size, size), flt)],
    )(at, back_sums, block_rates, segment_rates, *got)
    back_got = line_exchange(spread)
    chosen = kernel(
        functools.partial(choose_kernel, size),
        [state] * heads + [shape((heads, size, size), half)], 1 << 20, 1 << 20, "choose",
        scratch_shapes=[pltpu.VMEM((heads, size, size), flt)],
    )(at, *back_got)
    back_bf = chosen[-1]
    owned = [chosen[0]] + [
        along_users(chosen[place], place // CORES, place % CORES) for place in range(1, users)
    ]

    packed = kernel(
        functools.partial(pack_kernel, size),
        shape((heads, length + size + EXTRA, size)), 1 << 20, 3 << 20, "pack", False,
    )(d_output, state_in, rates)
    every = lax.all_to_all(packed, "batch", 0, 0)

    all_rows, head_qkv = pl.pallas_call(
        recall_kernel,
        grid_spec=pltpu.PrefetchScalarGridSpec(
            num_scalar_prefetch=1,
            grid=(chips,),
            in_specs=[pl.BlockSpec((1, length, width), lambda i, at: (i, 0, 0))] * 2
            + [
                pl.BlockSpec((width, size), lambda i, at, part=part: (0, part * heads + at[0]))
                for part in range(3)
            ],
            out_specs=[
                pl.BlockSpec((CORES, length, width), lambda i, at: (i, 0, 0)),
                pl.BlockSpec((CORES, length, 3 * size), lambda i, at: (i, 0, 0)),
            ],
        ),
        out_shape=[shape((users, length, width), half), shape((users, length, 3 * size), half)],
        compiler_params=pltpu.CompilerParams(vmem_limit_bytes=16 << 20),
        cost_estimate=pl.CostEstimate(
            flops=6 * length * width * width, bytes_accessed=14 << 20, transcendentals=0
        ),
        name="recall",
    )(at, rows_mine, rows_other, qkv_weight, qkv_weight, qkv_weight)

    owner_tall, turned_query, key_inner, value_inner = kernel(
        functools.partial(owner_kernel, size),
        [shape((length, users)), shape((size, users * length), half)] + [shape((users, length, size))] * 2,
        users * 12 * square, 6 << 20, "owner", False,
    )(head_qkv, every)
    turned_pair = kernel(
        functools.partial(late_kernel, size),
        shape((2 * size, users * length), half), users * 2 * square, 4 << 20, "late",
        scratch_shapes=[pltpu.VMEM((users, size, size), half)],
    )(at, head_qkv, key_inner, value_inner, owner_tall, *owned)

    def term(step):
        return kernel(
            functools.partial(term_kernel, size, step, segments),
            shape((3 * size, width // segments)),
            6 * users * length * size * width // segments, 3 << 20, "term",
        )(at, turned_query, turned_pair, all_rows)

    got = [along_segments(term(step), step) for step in (2, 1, 3)] + [term(0)]
    pieces = kernel(
        fold_kernel, [shape((width // count, 3 * size))] * heads, 1 << 20, 2 << 20, "fold",
        scratch_shapes=[pltpu.VMEM((heads, width // count, 3 * size), flt)],
    )(at, *got)
    got = line_exchange(pieces)
    mine = kernel(gather_kernel, shape((width // count, 3 * size)), 1 << 18, 1 << 18, "gather", False)(*got)

    other = along_users(mine, 0, 1)
    both = kernel(both_kernel, shape((CORES, width // count, 3 * size)), 1 << 16, 1 << 17, "both", False)(mine, other)
    summed = [both] + [along_users(both, step, 0) for step in range(1, chips)]
    squares = kernel(square_kernel, shape((count, EXTRA, size)), 1 << 18, 1 << 18, "square", False)(*summed)
    squares = lax.all_to_all(squares, "seq", 0, 0)
    weight_step = kernel(
        step_kernel, shape((width // count, 3 * width)), 1 << 18, 1 << 20, "step",
        scratch_shapes=[pltpu.VMEM((heads, width // count, 3 * size), flt)],
    )(at, squares, *summed)

    d_query, key_part, value_part = kernel(
        functools.partial(inner_kernel, size),
        [tokens(half), tokens(flt), tokens(flt)], heads * 10 * square, 6 << 20, "inner", False,
    )(q, k, v, d_output, weights, state_in, tall, flat)
    weight_rows = lambda part: pl.BlockSpec((wide, width), lambda i: (i, part))
    d_rows = pl.pallas_call(
        functools.partial(rows_kernel, size),
        grid=(pairs,),
        in_specs=[whole((length, width))] * 5
        + [whole((heads, size, size)), whole((length, heads))]
        + [weight_rows(part) for part in range(3)],
        out_specs=column,
        out_shape=tokens(half),
        scratch_shapes=[pltpu.VMEM((length, width), half)] * 2,
        compiler_params=pltpu.CompilerParams(vmem_limit_bytes=24 << 20),
        cost_estimate=pl.CostEstimate(
            flops=6 * length * width * width, bytes_accessed=8 * width * width, transcendentals=0
        ),
        name="rows",
    )(d_query, key_part, value_part, k, v, back_bf, tall, qkv_weight, qkv_weight, qkv_weight)
    return (mixed[None], d_rows[None], weight_step)


def solution(mesh):
    placed = (P("batch", "seq", None), P("batch", None, "seq"), P(), P("batch", "seq", None))
    return jax.shard_map(
        on_device,
        mesh=mesh,
        in_specs=placed,
        out_specs=(P("batch", "seq", None), P("batch", "seq", None), P("seq", None)),
        check_vma=False,
    )
```

```python
import functools

import jax
import jax.numpy as jnp
from jax import lax
from jax.experimental import pallas as pl
from jax.experimental.pallas import tpu as pltpu
from jax.sharding import PartitionSpec as P

epsilon = 1e-06
flt = jnp.float32
half = jnp.bfloat16
PAIR = 2
CORES = 2
EXTRA = 8
ORDER = ((0, 0), (1, 0), (3, 0), (2, 0), (0, 1), (1, 1), (2, 1), (3, 1))
FIRST = 3


def dot(a, b, ca, cb, precision=None):
    return lax.dot_general(
        a, b, (((ca,), (cb,)), ((), ())), preferred_element_type=flt, precision=precision
    )


def ordered(length):
    at = lax.broadcasted_iota(jnp.int32, (length, length), 0)
    source = lax.broadcasted_iota(jnp.int32, (length, length), 1)
    return at >= source


def running(rates):
    ones = ordered(rates.shape[1]).astype(flt)
    exact = lax.Precision.HIGHEST
    return dot(ones, rates, 1, 1, exact), dot(rates, ones, 1, 1, exact)


def decay_within(tall, flat, index):
    length = tall.shape[0]
    causal = ordered(length)
    spread = tall[:, index : index + 1] - flat[index : index + 1, :]
    return jnp.where(causal, jnp.exp(jnp.where(causal, spread, 0.0)), 0.0)


def place_in(index, step, count):
    return lax.rem(index + step + count, count)


def put_sum(sent_ref, lane, total):
    pieces = sent_ref.shape[0] // PAIR
    share = total.shape[0] // pieces
    for piece in range(pieces):
        sent_ref[lane * pieces + piece, :share, :] = total[piece * share : (piece + 1) * share]


def project_kernel(size, at_ref, rows_ref, wq_ref, wk_ref, wv_ref, rates_ref, q_ref, k_ref, v_ref,
                   tall_ref, flat_ref, sent_ref, top_ref, low_ref, own_ref, leaving_ref):
    step = pl.program_id(0)
    rows = rows_ref[...]
    width = top_ref.shape[1] // pl.num_programs(0)
    middle = top_ref.shape[0]
    columns = pl.ds(pl.multiple_of(step * width, width), width)
    top_ref[:, columns] = rows_ref[:middle, columns].astype(flt)
    low_ref[:, columns] = rows_ref[middle:, columns].astype(flt)
    for lane in range(PAIR):

        @pl.when(at_ref[0] == step * PAIR + lane)
        def _():
            for part, weight_ref in enumerate((wq_ref, wk_ref, wv_ref)):
                own_ref[:, part * size : (part + 1) * size] = weight_ref[:, lane * size : (lane + 1) * size]

    @pl.when(step == 0)
    def _():
        tall, flat = running(rates_ref[...])
        tall_ref[...] = tall
        flat_ref[...] = flat
        leaving_ref[...] = jnp.exp(tall[-1:] - tall)

    k = dot(rows, wk_ref[...], 1, 0).astype(half)
    v = dot(rows, wv_ref[...], 1, 0).astype(half)
    k_ref[...] = k
    v_ref[...] = v
    leaving = leaving_ref[...]
    lanes = lax.broadcasted_iota(jnp.int32, leaving.shape, 1)
    pieces = sent_ref.shape[0] // PAIR
    share = sent_ref.shape[1] - EXTRA
    for lane in range(PAIR):
        at = slice(lane * size, (lane + 1) * size)
        head = step * PAIR + lane
        column = jnp.sum(jnp.where(lanes == head, leaving, 0.0), axis=1, keepdims=True)
        keyed = (k[:, at].astype(flt) * column).astype(half)
        put_sum(sent_ref, lane, dot(keyed, v[:, at], 0, 0))
        last = flat_ref[pl.ds(head, 1), :][:, -1:]
        rate = jnp.broadcast_to(jnp.exp(last), (EXTRA, size))
        for piece in range(pieces):
            sent_ref[lane * pieces + piece, share:, :] = rate
    q_ref[...] = dot(rows, wq_ref[...], 1, 0).astype(half)


def scan_kernel(got_ref, mark_ref, out_ref, rates_ref):
    count, share, columns = out_ref.shape
    state = jnp.zeros((share, columns), flt)
    for block in range(count):
        out_ref[block] = state
        rates_ref[block] = got_ref[block, share:, :]
        state = got_ref[block, share : share + 1, :] * state + got_ref[block, :share, :]


def back_scan_kernel(got_ref, rates_ref, after_ref, out_ref, mark_ref):
    count, share, columns = out_ref.shape
    mark_ref[...] = after_ref[...] * 0.0
    state = jnp.zeros((share, columns), flt)
    for block in range(count - 1, -1, -1):
        out_ref[block] = state
        state = rates_ref[block, :1, :] * state + got_ref[block]


def weights_kernel(heads, size, q_ref, k_ref, v_ref, tall_ref, flat_ref, weights_ref, intra_ref):
    tall, flat = tall_ref[...], flat_ref[...]
    for head in range(heads):
        at = slice(head * size, (head + 1) * size)
        scores = dot(q_ref[:, at], k_ref[:, at], 1, 1)
        weights = (scores * decay_within(tall, flat, head)).astype(half)
        weights_ref[head] = weights
        intra_ref[:, at] = dot(weights, v_ref[:, at], 1, 0)


def mix_kernel(size, q_ref, intra_ref, up_ref, tall_ref, state_ref, after_ref, mixed_ref, dout_ref, sent_ref):
    heads = state_ref.shape[0]
    pieces = sent_ref.shape[0] // heads
    share = size // pieces
    entering = jnp.exp(tall_ref[...])
    for head in range(heads):
        at = slice(head * size, (head + 1) * size)
        q = q_ref[:, at]
        column = entering[:, head : head + 1]
        output = intra_ref[:, at] + dot(q, state_ref[head].astype(half), 1, 0) * column
        scale = lax.rsqrt(jnp.mean(output * output, axis=-1, keepdims=True) + epsilon)
        normed = output * scale
        mixed_ref[:, at] = normed.astype(half)
        incoming = up_ref[:, at].astype(flt)
        along = jnp.mean(normed * incoming, axis=-1, keepdims=True)
        d_output = (scale * (incoming - normed * along)).astype(half)
        dout_ref[:, at] = d_output
        lifted = (q.astype(flt) * column).astype(half)
        total = dot(lifted, d_output, 0, 0)
        for piece in range(pieces):
            sent_ref[head * pieces + piece] = total[piece * share : (piece + 1) * share]


def head_at(at_ref, step, turn, chips):
    chip, core = at_ref[0] // CORES, lax.rem(at_ref[0], CORES)
    return place_in(chip, step, chips) * CORES + lax.rem(core + turn, CORES)


def pack_kernel(size, at_ref, dout_ref, state_ref, rates_ref, own_ref, other_ref):
    length = dout_ref.shape[0]
    chips = own_ref.shape[0]
    for turn, out_ref in enumerate((own_ref, other_ref)):
        for step in range(chips):
            head = head_at(at_ref, step, turn, chips)
            columns = pl.ds(pl.multiple_of(head * size, size), size)
            out_ref[step, :length, :] = dout_ref[:, columns].astype(flt)
            out_ref[step, length : length + size, :] = state_ref[head]
            row = rates_ref[pl.ds(head, 1), :]
            out_ref[step, length + size :, :] = jnp.zeros((EXTRA, size), flt)
            for part in range(length // size):
                to = length + size + part
                out_ref[step, to : to + 1, :] = row[:, part * size : (part + 1) * size]


def pair_kernel(own_ref, came_ref, *out_refs):
    for step, out_ref in enumerate(out_refs):
        out_ref[0] = own_ref[step]
        out_ref[1] = came_ref[step]


def recall_kernel(weight_ref, after_ref, *refs):
    wide_refs, (rows_ref, qkv_ref, mark_ref, held_ref, sem) = refs[:-5], refs[-5:]
    count, length, _ = rows_ref.shape
    middle = length // 2
    copies = [
        pltpu.make_async_copy(wide_ref, held_ref.at[part // 2, pl.ds(part % 2 * middle, middle)], sem.at[part])
        for part, wide_ref in enumerate(wide_refs)
    ]
    for copy in copies:
        copy.start()
    mark_ref[...] = jnp.zeros(mark_ref.shape, flt)
    for place in range(count):
        copies[2 * place].wait()
        copies[2 * place + 1].wait()
        rows_ref[place] = held_ref[place].astype(half)
        qkv_ref[place] = dot(rows_ref[place], weight_ref[...], 1, 0).astype(half)


def inner_grads(q, k, v, d_output, weights, state, within, entering):
    d_score = (dot(d_output, v, 1, 1) * within).astype(half)
    d_query = dot(d_score, k, 1, 0) + entering * dot(d_output, state, 1, 1)
    return d_query.astype(half), dot(d_score, q, 0, 0), dot(weights, d_output, 0, 0)


def owner_kernel(size, first_ref, rest_ref, *refs):
    got_refs, (tall_ref, turned_ref, dk_ref, dv_ref) = refs[:-4], refs[-4:]
    length = first_ref.shape[1]
    base = length + size
    gots = [got_refs[step].at[turn] for step, turn in ORDER]
    rates = jnp.concatenate(
        [
            jnp.concatenate([got[base + part : base + part + 1, :] for part in range(length // size)], axis=1)
            for got in gots
        ],
        axis=0,
    )
    tall, flat = running(rates)
    tall_ref[...] = tall
    entering = jnp.exp(tall)
    for place, got in enumerate(gots):
        qkv = first_ref[place] if place < FIRST else rest_ref[place - FIRST]
        q, k, v = (qkv[:, part * size : (part + 1) * size] for part in range(3))
        within = decay_within(tall, flat, place)
        weights = (dot(q, k, 1, 1) * within).astype(half)
        d_output = got[:length, :].astype(half)
        state = got[length:base, :].astype(half)
        d_query, dk_ref[place], dv_ref[place] = inner_grads(
            q, k, v, d_output, weights, state, within, entering[:, place : place + 1]
        )
        turned_ref[:, place * length : (place + 1) * length] = d_query.T


def late_kernel(size, first_ref, rest_ref, dk_ref, dv_ref, tall_ref, *refs):
    back_refs, out_ref = refs[:-1], refs[-1]
    length = first_ref.shape[1]
    tall = tall_ref[...]
    leaving = jnp.exp(tall[-1:] - tall)
    for place, (step, turn) in enumerate(ORDER):
        at = slice(place * length, (place + 1) * length)
        column = leaving[:, place : place + 1]
        qkv_ref = first_ref.at[place] if place < FIRST else rest_ref.at[place - FIRST]
        k = qkv_ref[:, size : 2 * size]
        v = qkv_ref[:, 2 * size :]
        back = back_refs[step][turn].astype(half)
        d_key = (dk_ref[place] + column * dot(v, back, 1, 1)).astype(half)
        d_value = (dv_ref[place] + column * dot(k, back, 1, 0)).astype(half)
        out_ref[:size, at] = d_key.T
        out_ref[size:, at] = d_value.T


def choose_kernel(at_ref, back_ref, after_ref, own_ref, other_ref, keep_ref):
    chips = own_ref.shape[0]
    for step in range(chips):
        own_ref[step] = back_ref[head_at(at_ref, step, 0, chips)]
        other_ref[step] = back_ref[head_at(at_ref, step, 1, chips)]
    keep_ref[...] = back_ref[...].astype(half)


def term_kernel(step, at_ref, dq_ref, dkv_ref, first_ref, rest_ref, out_ref):
    _, length, width = first_ref.shape
    users = len(ORDER)
    size, share = dq_ref.shape[0], out_ref.shape[1]
    target = place_in(at_ref[1] // users, step, width // share)
    columns = pl.ds(pl.multiple_of(target * share, share), share)
    middle = FIRST * length
    first = first_ref[:, :, columns].reshape(middle, share)
    rest = rest_ref[:, :, columns].reshape(users * length - middle, share)
    out_ref[:size, :] = dot(dq_ref[:, :middle], first, 1, 0) + dot(dq_ref[:, middle:], rest, 1, 0)
    out_ref[size:, :] = dot(dkv_ref[:, :middle], first, 1, 0) + dot(dkv_ref[:, middle:], rest, 1, 0)


def fold_kernel(at_ref, *refs):
    got_refs, out_refs, slots_ref = refs[:4], refs[5:-1], refs[-1]
    blocks = len(out_refs)
    total = got_refs[0][...]
    for got_ref in got_refs[1:]:
        total += got_ref[...]
    turned = total.T
    line = lax.rem(at_ref[1], blocks)
    share = turned.shape[0] // blocks
    for block in range(blocks):
        slots_ref[block] = turned[block * share : (block + 1) * share]
    for step, out_ref in enumerate(out_refs):
        out_ref[...] = slots_ref[place_in(line, step, blocks)]


def gather_kernel(*refs):
    total = refs[0][...]
    for got_ref in refs[1:-1]:
        total += got_ref[...]
    refs[-1][...] = total


def both_kernel(mine_ref, other_ref, out_ref):
    out_ref[0] = mine_ref[...]
    out_ref[1] = other_ref[...]


def square_kernel(*refs):
    got_refs, out_ref = refs[:-1], refs[-1]
    size = out_ref.shape[2]
    for part in range(3):
        total = jnp.zeros((1, size), flt)
        for got_ref in got_refs:
            for core in range(CORES):
                piece = got_ref[core, :, part * size : (part + 1) * size]
                total += jnp.sum(piece * piece, axis=0, keepdims=True)
        out_ref[:, part : part + 1, :] = jnp.broadcast_to(total[None], (out_ref.shape[0], 1, size))
    out_ref[:, 3:, :] = jnp.zeros((out_ref.shape[0], EXTRA - 3, size), flt)


def step_kernel(at_ref, squares_ref, *refs):
    got_refs, out_ref, slots_ref = refs[:-2], refs[-2], refs[-1]
    heads, share, width = slots_ref.shape
    size = width // 3
    chips = heads // CORES
    chip, core = at_ref[0] // CORES, lax.rem(at_ref[0], CORES)
    for step, got_ref in enumerate(got_refs):
        for turn in range(CORES):
            head = place_in(chip, -step, chips) * CORES + lax.rem(core + turn, CORES)
            slots_ref[head] = got_ref[turn]
    total = jnp.sum(squares_ref[...], axis=0)
    entries = float(heads * size) ** 2
    for part in range(3):
        mean = jnp.sum(total[part : part + 1], axis=1, keepdims=True) / entries
        factor = lax.rsqrt(mean + epsilon)
        for head in range(heads):
            at = (part * heads + head) * size
            out_ref[:, at : at + size] = slots_ref[head, :, part * size : (part + 1) * size] * factor


def rows_kernel(size, dq_ref, dki_ref, dvi_ref, k_ref, v_ref, back_ref, tall_ref,
                wq_ref, wk_ref, wv_ref, out_ref, dk_ref, dv_ref):
    @pl.when(pl.program_id(0) == 0)
    def _():
        tall = tall_ref[...]
        leaving = jnp.exp(tall[-1:] - tall)
        for head in range(back_ref.shape[0]):
            at = slice(head * size, (head + 1) * size)
            column = leaving[:, head : head + 1]
            back = back_ref[head]
            dk_ref[:, at] = (dki_ref[:, at] + column * dot(v_ref[:, at], back, 1, 1)).astype(half)
            dv_ref[:, at] = (dvi_ref[:, at] + column * dot(k_ref[:, at], back, 1, 0)).astype(half)

    total = dot(dq_ref[...], wq_ref[...], 1, 1)
    total += dot(dk_ref[...], wk_ref[...], 1, 1)
    total += dot(dv_ref[...], wv_ref[...], 1, 1)
    out_ref[...] = total.astype(half)


def inner_kernel(size, q_ref, k_ref, v_ref, dout_ref, weights_ref, state_ref, tall_ref, flat_ref,
                 dq_ref, dk_ref, dv_ref):
    tall, flat = tall_ref[...], flat_ref[...]
    entering = jnp.exp(tall)
    for head in range(weights_ref.shape[0]):
        at = slice(head * size, (head + 1) * size)
        dq_ref[:, at], dk_ref[:, at], dv_ref[:, at] = inner_grads(
            q_ref[:, at], k_ref[:, at], v_ref[:, at], dout_ref[:, at], weights_ref[head],
            state_ref[head].astype(half), decay_within(tall, flat, head), entering[:, head : head + 1]
        )


def shape(dims, kind=flt):
    return jax.ShapeDtypeStruct(dims, kind)


def kernel(body, out_shape, flops, moved, name, placed=True, limit=16, after=None, **more):
    cost = pl.CostEstimate(flops=int(flops), bytes_accessed=int(moved), transcendentals=0)
    settings = dict(
        out_shape=out_shape,
        compiler_params=pltpu.CompilerParams(vmem_limit_bytes=limit << 20),
        cost_estimate=cost,
        name=name,
    )
    settings.update(more)

    def space(place):
        if after is not None and place >= after:
            return pl.ANY
        return pltpu.SMEM if placed and place == 0 else pltpu.VMEM

    return lambda *arrays: pl.pallas_call(
        body,
        in_specs=[pl.BlockSpec(memory_space=space(place)) for place in range(len(arrays))],
        **settings,
    )(*arrays)


def on_device(behaviors, log_decay, qkv_weight, cotangent):
    rows = behaviors[0]
    rates = log_decay[0]
    upstream = cotangent[0]
    length, width = rows.shape
    heads = rates.shape[0]
    size = width // heads
    users = lax.axis_size("batch")
    count = lax.axis_size("seq")
    segments = count // heads
    chips = users // CORES
    pairs = heads // PAIR
    wide = PAIR * size
    at = jnp.stack([lax.axis_index("batch"), lax.axis_index("seq")]).astype(jnp.int32)

    def along_line(array, step):
        pairs_of = [(s, s // heads * heads + (s + step) % heads) for s in range(count)]
        return lax.ppermute(array, "seq", pairs_of)

    def along_segments(array, step):
        return lax.ppermute(array, "seq", [(s, (s + step * heads) % count) for s in range(count)])

    def along_users(array, step, turn):
        pairs_of = [
            (u, (u // CORES + step) % chips * CORES + (u + turn) % CORES) for u in range(users)
        ]
        return lax.ppermute(array, "batch", pairs_of)

    def line_exchange(arrays):
        return [arrays[0]] + [along_line(arrays[step], step) for step in range(1, heads)]

    whole = lambda dims: pl.BlockSpec(dims, lambda i: (0,) * len(dims))
    column = pl.BlockSpec((length, wide), lambda i: (0, i))
    weight_at = lambda part: pl.BlockSpec((width, wide), lambda i: (0, part * pairs + i))
    tokens = lambda kind: shape((length, width), kind)
    state = shape((size, size))
    smem = pl.BlockSpec(memory_space=pltpu.SMEM)
    share = heads * size // count
    slices = shape((count, share, size))
    square = length * length * size

    def exchange(own, other, moved):
        dims = own.shape[1:]
        came = along_users(other, 0, 1)
        both = kernel(
            pair_kernel, [shape((CORES,) + dims)] * chips, 1 << 16, moved, "pair", False
        )(own, came)
        return [both[0]] + [along_users(both[step], step, 0) for step in range(1, chips)]

    q, k, v, tall, flat, sums, top, low, weight_columns = pl.pallas_call(
        functools.partial(project_kernel, size),
        grid=(pairs,),
        in_specs=[smem, whole((length, width)), weight_at(0), weight_at(1), weight_at(2), whole((heads, length))],
        out_specs=[column] * 3 + [whole((length, heads)), whole((heads, length))]
        + [pl.BlockSpec((count // pairs, share + EXTRA, size), lambda i: (i, 0, 0))]
        + [whole((length // 2, width))] * 2 + [whole((width, 3 * size))],
        out_shape=[tokens(half)] * 3 + [shape((length, heads)), shape((heads, length))]
        + [shape((count, share + EXTRA, size))] + [shape((length // 2, width))] * 2
        + [shape((width, 3 * size), half)],
        scratch_shapes=[pltpu.VMEM((length, heads), flt)],
        compiler_params=pltpu.CompilerParams(vmem_limit_bytes=59 << 20),
        cost_estimate=pl.CostEstimate(
            flops=6 * length * width * width, bytes_accessed=8 * width * width, transcendentals=0
        ),
        name="project",
    )(at, rows, qkv_weight, qkv_weight, qkv_weight, rates)
    ahead, astern = (lambda array: along_users(array, 1, 0)), (lambda array: along_users(array, chips - 1, 0))
    top_before, low_behind = ahead(top), astern(low)
    low_before, top_behind = ahead(low), astern(top)
    top_beyond, low_beyond = ahead(top_before), astern(low_behind)
    near_wide = [top, low, top_before, low_before, top_beyond, low_beyond, top_behind, low_behind]
    far_wide = [along_users(array, 0, 1) for array in near_wide]

    def mark_of(*arrays):
        return sum(array[-EXTRA:, :size] for array in arrays)

    got = lax.all_to_all(sums, "seq", 0, 0)
    entered, block_rates = kernel(
        scan_kernel, [slices, shape((count, EXTRA, size))], 1 << 18, 1 << 20, "scan", False
    )(got, mark_of(top_before, low_behind))
    state_in = lax.all_to_all(entered, "seq", 0, 0).reshape(heads, size, size)

    weights, intra = kernel(
        functools.partial(weights_kernel, heads, size),
        [shape((heads, length, length), half), tokens(flt)],
        heads * 4 * square, 5 << 20, "weights", False,
    )(q, k, v, tall, flat)

    mixed, d_output, sums = kernel(
        functools.partial(mix_kernel, size),
        [tokens(half), tokens(half), slices],
        heads * 2 * square, 5 << 20, "mix", False,
    )(q, intra, upstream, tall, state_in, mark_of(low_before, top_behind))
    got = lax.all_to_all(sums, "seq", 0, 0)
    packed = kernel(
        functools.partial(pack_kernel, size),
        [shape((chips, length + size + EXTRA, size))] * CORES, 1 << 18, 3 << 20, "pack",
    )(at, d_output, state_in, rates)
    every = exchange(*packed, 3 << 20)

    def recall(wide, after, name):
        count = len(wide) // 2
        return kernel(
            recall_kernel,
            [shape((count, length, width), half), shape((count, length, 3 * size), half), shape((EXTRA, size))],
            6 * length * width * size * count, 8 << 20, name, False, after=2, limit=50,
            scratch_shapes=[pltpu.VMEM((count, length, width), flt), pltpu.SemaphoreType.DMA((2 * count,))],
        )(weight_columns, after, *wide)

    pieces = {(step, 0): near_wide[2 * step : 2 * step + 2] for step in range(chips)}
    pieces.update({(step, 1): far_wide[2 * step : 2 * step + 2] for step in range(chips)})
    wides = [piece for place in ORDER for piece in pieces[place]]
    first_rows, first_qkv, mark = recall(wides[: 2 * FIRST], mark_of(top_before), "recall")

    entered, mark = kernel(
        back_scan_kernel, [slices, shape((EXTRA, size))], 1 << 18, 1 << 20, "back_scan", False
    )(got, block_rates, mark + mark_of(top_beyond, low_beyond))
    back = lax.all_to_all(entered, "seq", 0, 0).reshape(heads, size, size)
    d_query, key_part, value_part = kernel(
        functools.partial(inner_kernel, size),
        [tokens(half), tokens(flt), tokens(flt)], heads * 10 * square, 6 << 20, "inner", False,
    )(q, k, v, d_output, weights, state_in, tall, flat)
    rest_rows, rest_qkv, mark = recall(wides[2 * FIRST :], mark, "recall_rest")
    *chosen, back_bf = kernel(
        choose_kernel, [shape((chips, size, size))] * CORES + [shape((heads, size, size), half)],
        1 << 18, 1 << 20, "choose",
    )(at, back, mark)
    owned = exchange(*chosen, 1 << 20)

    owner_tall, turned_query, key_inner, value_inner = kernel(
        functools.partial(owner_kernel, size),
        [shape((length, users)), shape((size, users * length), half)] + [shape((users, length, size))] * 2,
        users * 12 * square, 6 << 20, "owner", False,
    )(first_qkv, rest_qkv, *every)
    turned_pair = kernel(
        functools.partial(late_kernel, size),
        shape((2 * size, users * length), half), users * 2 * square, 4 << 20, "late", False,
    )(first_qkv, rest_qkv, key_inner, value_inner, owner_tall, *owned)

    weight_rows = lambda part: pl.BlockSpec((wide, width), lambda i: (i, part))
    d_rows = pl.pallas_call(
        functools.partial(rows_kernel, size),
        grid=(pairs,),
        in_specs=[whole((length, width))] * 5
        + [whole((heads, size, size)), whole((length, heads))]
        + [weight_rows(part) for part in range(3)],
        out_specs=column,
        out_shape=tokens(half),
        scratch_shapes=[pltpu.VMEM((length, width), half)] * 2,
        compiler_params=pltpu.CompilerParams(vmem_limit_bytes=24 << 20),
        cost_estimate=pl.CostEstimate(
            flops=6 * length * width * width, bytes_accessed=8 * width * width, transcendentals=0
        ),
        name="rows",
    )(d_query, key_part, value_part, k, v, back_bf, tall, qkv_weight, qkv_weight, qkv_weight)
    def term(step):
        return kernel(
            functools.partial(term_kernel, step),
            shape((3 * size, width // segments)),
            6 * users * length * size * width // segments, 3 << 20, "term",
        )(at, turned_query, turned_pair, first_rows, rest_rows)

    got = [along_segments(term(step), step) for step in (2, 1, 3)] + [term(0)]
    pieces = kernel(
        fold_kernel, [shape((width // count, 3 * size))] * heads, 1 << 20, 2 << 20, "fold",
        scratch_shapes=[pltpu.VMEM((heads, width // count, 3 * size), flt)], after=5,
    )(at, *got, d_rows)
    got = line_exchange(pieces)
    mine = kernel(gather_kernel, shape((width // count, 3 * size)), 1 << 18, 1 << 18, "gather", False)(*got)

    other = along_users(mine, 0, 1)
    both = kernel(both_kernel, shape((CORES, width // count, 3 * size)), 1 << 16, 1 << 17, "both", False)(mine, other)
    summed = [both] + [along_users(both, step, 0) for step in range(1, chips)]
    squares = kernel(square_kernel, shape((count, EXTRA, size)), 1 << 18, 1 << 18, "square", False)(*summed)
    squares = lax.all_to_all(squares, "seq", 0, 0)
    weight_step = kernel(
        step_kernel, shape((width // count, 3 * width)), 1 << 18, 1 << 20, "step",
        scratch_shapes=[pltpu.VMEM((heads, width // count, 3 * size), flt)],
    )(at, squares, *summed)

    return (mixed[None], d_rows[None], weight_step)


def solution(mesh):
    placed = (P("batch", "seq", None), P("batch", None, "seq"), P(), P("batch", "seq", None))
    return jax.shard_map(
        on_device,
        mesh=mesh,
        in_specs=placed,
        out_specs=(P("batch", "seq", None), P("batch", "seq", None), P("seq", None)),
        check_vma=False,
    )
```

```python
import functools

import jax
import jax.numpy as jnp
from jax import lax
from jax.experimental import pallas as pl
from jax.experimental.pallas import tpu as pltpu
from jax.sharding import PartitionSpec as P

epsilon = 1e-06
flt = jnp.float32
half = jnp.bfloat16
PAIR = 2
CORES = 2
EXTRA = 8
ORDER = ((0, 0), (1, 0), (3, 0), (2, 0), (0, 1), (1, 1), (2, 1), (3, 1))
FIRST = 3


def dot(a, b, ca, cb, precision=None):
    return lax.dot_general(
        a, b, (((ca,), (cb,)), ((), ())), preferred_element_type=flt, precision=precision
    )


def ordered(length):
    at = lax.broadcasted_iota(jnp.int32, (length, length), 0)
    source = lax.broadcasted_iota(jnp.int32, (length, length), 1)
    return at >= source


def running(rates):
    ones = ordered(rates.shape[1]).astype(flt)
    exact = lax.Precision.HIGHEST
    return dot(ones, rates, 1, 1, exact), dot(rates, ones, 1, 1, exact)


def decay_within(tall, flat, index):
    length = tall.shape[0]
    causal = ordered(length)
    spread = tall[:, index : index + 1] - flat[index : index + 1, :]
    return jnp.where(causal, jnp.exp(jnp.where(causal, spread, 0.0)), 0.0)


def place_in(index, step, count):
    return lax.rem(index + step + count, count)


def put_sum(sent_ref, lane, total):
    pieces = sent_ref.shape[0] // PAIR
    share = total.shape[0] // pieces
    for piece in range(pieces):
        sent_ref[lane * pieces + piece, :share, :] = total[piece * share : (piece + 1) * share]


def project_kernel(size, at_ref, rows_ref, wq_ref, wk_ref, wv_ref, rates_ref, q_ref, k_ref, v_ref,
                   tall_ref, flat_ref, sent_ref, top_ref, low_ref, own_ref, leaving_ref):
    step = pl.program_id(0)
    rows = rows_ref[...]
    width = top_ref.shape[1] // pl.num_programs(0)
    middle = top_ref.shape[0]
    columns = pl.ds(pl.multiple_of(step * width, width), width)
    top_ref[:, columns] = rows_ref[:middle, columns].astype(flt)
    low_ref[:, columns] = rows_ref[middle:, columns].astype(flt)
    for lane in range(PAIR):

        @pl.when(at_ref[0] == step * PAIR + lane)
        def _():
            for part, weight_ref in enumerate((wq_ref, wk_ref, wv_ref)):
                own_ref[:, part * size : (part + 1) * size] = weight_ref[:, lane * size : (lane + 1) * size]

    @pl.when(step == 0)
    def _():
        tall, flat = running(rates_ref[...])
        tall_ref[...] = tall
        flat_ref[...] = flat
        leaving_ref[...] = jnp.exp(tall[-1:] - tall)

    k = dot(rows, wk_ref[...], 1, 0).astype(half)
    v = dot(rows, wv_ref[...], 1, 0).astype(half)
    k_ref[...] = k
    v_ref[...] = v
    leaving = leaving_ref[...]
    lanes = lax.broadcasted_iota(jnp.int32, leaving.shape, 1)
    pieces = sent_ref.shape[0] // PAIR
    share = sent_ref.shape[1] - EXTRA
    for lane in range(PAIR):
        at = slice(lane * size, (lane + 1) * size)
        head = step * PAIR + lane
        column = jnp.sum(jnp.where(lanes == head, leaving, 0.0), axis=1, keepdims=True)
        keyed = (k[:, at].astype(flt) * column).astype(half)
        put_sum(sent_ref, lane, dot(keyed, v[:, at], 0, 0))
        last = flat_ref[pl.ds(head, 1), :][:, -1:]
        rate = jnp.broadcast_to(jnp.exp(last), (EXTRA, size))
        for piece in range(pieces):
            sent_ref[lane * pieces + piece, share:, :] = rate
    q_ref[...] = dot(rows, wq_ref[...], 1, 0).astype(half)


def scan_kernel(got_ref, mark_ref, out_ref, rates_ref):
    count, share, columns = out_ref.shape
    state = jnp.zeros((share, columns), flt)
    for block in range(count):
        out_ref[block] = state
        rates_ref[block] = got_ref[block, share:, :]
        state = got_ref[block, share : share + 1, :] * state + got_ref[block, :share, :]


def back_scan_kernel(got_ref, rates_ref, after_ref, out_ref, mark_ref):
    count, share, columns = out_ref.shape
    mark_ref[...] = after_ref[...] * 0.0
    state = jnp.zeros((share, columns), flt)
    for block in range(count - 1, -1, -1):
        out_ref[block] = state
        state = rates_ref[block, :1, :] * state + got_ref[block]


def column_of(table, index):
    lanes = lax.broadcasted_iota(jnp.int32, table.shape, 1)
    return jnp.sum(jnp.where(lanes == index, table, 0.0), axis=1, keepdims=True)


def decay_at(tall, flat_ref, index):
    length = tall.shape[0]
    causal = ordered(length)
    spread = column_of(tall, index) - flat_ref[pl.ds(index, 1), :]
    return jnp.where(causal, jnp.exp(jnp.where(causal, spread, 0.0)), 0.0)


def lanes_at(head, size):
    return pl.ds(pl.multiple_of(head * size, size), size)


def weights_kernel(heads, size, q_ref, k_ref, v_ref, tall_ref, flat_ref, weights_ref, intra_ref):
    tall = tall_ref[...]

    def one(head, _):
        at = lanes_at(head, size)
        scores = dot(q_ref[:, at], k_ref[:, at], 1, 1)
        weights = (scores * decay_at(tall, flat_ref, head)).astype(half)
        weights_ref[head] = weights
        intra_ref[:, at] = dot(weights, v_ref[:, at], 1, 0)

    lax.fori_loop(0, heads, one, None)


def mix_kernel(size, q_ref, intra_ref, up_ref, tall_ref, state_ref, after_ref, mixed_ref, dout_ref, sent_ref):
    heads = state_ref.shape[0]
    pieces = sent_ref.shape[0] // heads
    share = size // pieces
    entering = jnp.exp(tall_ref[...])

    def one(head, _):
        at = lanes_at(head, size)
        q = q_ref[:, at]
        column = column_of(entering, head)
        output = intra_ref[:, at] + dot(q, state_ref[head].astype(half), 1, 0) * column
        scale = lax.rsqrt(jnp.mean(output * output, axis=-1, keepdims=True) + epsilon)
        normed = output * scale
        mixed_ref[:, at] = normed.astype(half)
        incoming = up_ref[:, at].astype(flt)
        along = jnp.mean(normed * incoming, axis=-1, keepdims=True)
        d_output = (scale * (incoming - normed * along)).astype(half)
        dout_ref[:, at] = d_output
        lifted = (q.astype(flt) * column).astype(half)
        total = dot(lifted, d_output, 0, 0)
        for piece in range(pieces):
            sent_ref[head * pieces + piece] = total[piece * share : (piece + 1) * share]

    lax.fori_loop(0, heads, one, None, unroll=2)


def head_at(at_ref, step, turn, chips):
    chip, core = at_ref[0] // CORES, lax.rem(at_ref[0], CORES)
    return place_in(chip, step, chips) * CORES + lax.rem(core + turn, CORES)


def pack_kernel(size, at_ref, dout_ref, state_ref, rates_ref, own_ref, other_ref):
    length = dout_ref.shape[0]
    chips = own_ref.shape[0]
    for turn, out_ref in enumerate((own_ref, other_ref)):
        for step in range(chips):
            head = head_at(at_ref, step, turn, chips)
            columns = pl.ds(pl.multiple_of(head * size, size), size)
            out_ref[step, :length, :] = dout_ref[:, columns].astype(flt)
            out_ref[step, length : length + size, :] = state_ref[head]
            row = rates_ref[pl.ds(head, 1), :]
            out_ref[step, length + size :, :] = jnp.zeros((EXTRA, size), flt)
            for part in range(length // size):
                to = length + size + part
                out_ref[step, to : to + 1, :] = row[:, part * size : (part + 1) * size]


def pair_kernel(own_ref, came_ref, *out_refs):
    for step, out_ref in enumerate(out_refs):
        out_ref[0] = own_ref[step]
        out_ref[1] = came_ref[step]


def recall_kernel(weight_ref, after_ref, *refs):
    wide_refs, (rows_ref, qkv_ref, mark_ref, held_ref, sem) = refs[:-5], refs[-5:]
    count, length, _ = rows_ref.shape
    middle = length // 2
    copies = [
        pltpu.make_async_copy(wide_ref, held_ref.at[part // 2, pl.ds(part % 2 * middle, middle)], sem.at[part])
        for part, wide_ref in enumerate(wide_refs)
    ]
    for copy in copies:
        copy.start()
    mark_ref[...] = jnp.zeros(mark_ref.shape, flt)

    def one(place, _):
        for part in range(2):
            target = held_ref.at[place, pl.ds(part * middle, middle)]
            pltpu.make_async_copy(wide_refs[0], target, sem.at[2 * place + part]).wait()
        rows = held_ref[place].astype(half)
        rows_ref[place] = rows
        qkv_ref[place] = dot(rows, weight_ref[...], 1, 0).astype(half)

    lax.fori_loop(0, count, one, None)


def inner_grads(q, k, v, d_output, weights, state, within, entering):
    d_score = (dot(d_output, v, 1, 1) * within).astype(half)
    d_query = dot(d_score, k, 1, 0) + entering * dot(d_output, state, 1, 1)
    return d_query.astype(half), dot(d_score, q, 0, 0), dot(weights, d_output, 0, 0)


def owner_kernel(size, first_ref, rest_ref, *refs):
    got_refs, (tall_ref, turned_ref, dk_ref, dv_ref, flat_held, got_held) = refs[:-6], refs[-6:]
    length = first_ref.shape[1]
    base = length + size
    gots = [got_refs[step].at[turn] for step, turn in ORDER]
    rates = jnp.concatenate(
        [
            jnp.concatenate([got[base + part : base + part + 1, :] for part in range(length // size)], axis=1)
            for got in gots
        ],
        axis=0,
    )
    tall, flat = running(rates)
    tall_ref[...] = tall
    flat_held[...] = flat
    for place, got in enumerate(gots):
        got_held[place] = got[:base, :]
    entering = jnp.exp(tall)

    def one(place, qkv):
        q, k, v = (qkv[:, part * size : (part + 1) * size] for part in range(3))
        within = decay_at(tall, flat_held, place)
        weights = (dot(q, k, 1, 1) * within).astype(half)
        d_output = got_held[place, :length, :].astype(half)
        state = got_held[place, length:, :].astype(half)
        d_query, dk_ref[place], dv_ref[place] = inner_grads(
            q, k, v, d_output, weights, state, within, column_of(entering, place)
        )
        turned_ref[:, lanes_at(place, length)] = d_query.T

    lax.fori_loop(0, FIRST, lambda place, _: one(place, first_ref[place]), None)
    lax.fori_loop(FIRST, len(ORDER), lambda place, _: one(place, rest_ref[place - FIRST]), None)


def late_kernel(size, first_ref, rest_ref, dk_ref, dv_ref, tall_ref, dq_ref, *refs):
    refs[-2][:size, :] = dq_ref[...]
    back_refs, (out_ref, held_ref) = refs[:-2], refs[-2:]
    length = first_ref.shape[1]
    tall = tall_ref[...]
    leaving = jnp.exp(tall[-1:] - tall)
    for place, (step, turn) in enumerate(ORDER):
        held_ref[place] = back_refs[step][turn].astype(half)

    def one(place, k, v):
        column = column_of(leaving, place)
        back = held_ref[place]
        d_key = (dk_ref[place] + column * dot(v, back, 1, 1)).astype(half)
        d_value = (dv_ref[place] + column * dot(k, back, 1, 0)).astype(half)
        out_ref[size : 2 * size, lanes_at(place, length)] = d_key.T
        out_ref[2 * size :, lanes_at(place, length)] = d_value.T

    def near(place, _):
        one(place, first_ref[place, :, size : 2 * size], first_ref[place, :, 2 * size :])

    def far(place, _):
        at = place - FIRST
        one(place, rest_ref[at, :, size : 2 * size], rest_ref[at, :, 2 * size :])

    lax.fori_loop(0, FIRST, near, None)
    lax.fori_loop(FIRST, len(ORDER), far, None)


def choose_kernel(at_ref, back_ref, after_ref, own_ref, other_ref, keep_ref):
    chips = own_ref.shape[0]
    for step in range(chips):
        own_ref[step] = back_ref[head_at(at_ref, step, 0, chips)]
        other_ref[step] = back_ref[head_at(at_ref, step, 1, chips)]
    keep_ref[...] = back_ref[...].astype(half)


def term_kernel(step, at_ref, turned_ref, first_ref, rest_ref, out_ref):
    _, length, width = first_ref.shape
    users = len(ORDER)
    share = out_ref.shape[1]
    target = place_in(at_ref[1] // users, step, width // share)
    columns = pl.ds(pl.multiple_of(target * share, share), share)
    middle = FIRST * length
    first = first_ref[:, :, columns].reshape(middle, share)
    rest = rest_ref[:, :, columns].reshape(users * length - middle, share)
    out_ref[...] = dot(turned_ref[:, :middle], first, 1, 0) + dot(turned_ref[:, middle:], rest, 1, 0)


def fold_kernel(at_ref, *refs):
    got_refs, out_refs, slots_ref = refs[:4], refs[5:-1], refs[-1]
    blocks = len(out_refs)
    total = got_refs[0][...]
    for got_ref in got_refs[1:]:
        total += got_ref[...]
    turned = total.T
    line = lax.rem(at_ref[1], blocks)
    share = turned.shape[0] // blocks
    for block in range(blocks):
        slots_ref[block] = turned[block * share : (block + 1) * share]
    for step, out_ref in enumerate(out_refs):
        out_ref[...] = slots_ref[place_in(line, step, blocks)]


def gather_kernel(*refs):
    total = refs[0][...]
    for got_ref in refs[1:-1]:
        total += got_ref[...]
    refs[-1][...] = total


def both_kernel(mine_ref, other_ref, out_ref):
    out_ref[0] = mine_ref[...]
    out_ref[1] = other_ref[...]


def square_kernel(*refs):
    got_refs, out_ref = refs[:-1], refs[-1]
    size = out_ref.shape[2]
    for part in range(3):
        total = jnp.zeros((1, size), flt)
        for got_ref in got_refs:
            for core in range(CORES):
                piece = got_ref[core, :, part * size : (part + 1) * size]
                total += jnp.sum(piece * piece, axis=0, keepdims=True)
        out_ref[:, part : part + 1, :] = jnp.broadcast_to(total[None], (out_ref.shape[0], 1, size))
    out_ref[:, 3:, :] = jnp.zeros((out_ref.shape[0], EXTRA - 3, size), flt)


def step_kernel(at_ref, squares_ref, *refs):
    got_refs, out_ref, slots_ref = refs[:-2], refs[-2], refs[-1]
    heads, share, width = slots_ref.shape
    size = width // 3
    chips = heads // CORES
    chip, core = at_ref[0] // CORES, lax.rem(at_ref[0], CORES)
    for step, got_ref in enumerate(got_refs):
        for turn in range(CORES):
            head = place_in(chip, -step, chips) * CORES + lax.rem(core + turn, CORES)
            slots_ref[head] = got_ref[turn]
    total = jnp.sum(squares_ref[...], axis=0)
    entries = float(heads * size) ** 2
    for part in range(3):
        mean = jnp.sum(total[part : part + 1], axis=1, keepdims=True) / entries
        factor = lax.rsqrt(mean + epsilon)
        for head in range(heads):
            at = (part * heads + head) * size
            out_ref[:, at : at + size] = slots_ref[head, :, part * size : (part + 1) * size] * factor


def rows_kernel(size, dq_ref, dki_ref, dvi_ref, k_ref, v_ref, back_ref, tall_ref,
                wq_ref, wk_ref, wv_ref, out_ref, dk_ref, dv_ref):
    @pl.when(pl.program_id(0) == 0)
    def _():
        tall = tall_ref[...]
        leaving = jnp.exp(tall[-1:] - tall)
        for head in range(back_ref.shape[0]):
            at = slice(head * size, (head + 1) * size)
            column = leaving[:, head : head + 1]
            back = back_ref[head]
            dk_ref[:, at] = (dki_ref[:, at] + column * dot(v_ref[:, at], back, 1, 1)).astype(half)
            dv_ref[:, at] = (dvi_ref[:, at] + column * dot(k_ref[:, at], back, 1, 0)).astype(half)

    total = dot(dq_ref[...], wq_ref[...], 1, 1)
    total += dot(dk_ref[...], wk_ref[...], 1, 1)
    total += dot(dv_ref[...], wv_ref[...], 1, 1)
    out_ref[...] = total.astype(half)


def inner_kernel(size, q_ref, k_ref, v_ref, dout_ref, weights_ref, state_ref, tall_ref, flat_ref,
                 dq_ref, dk_ref, dv_ref):
    tall = tall_ref[...]
    entering = jnp.exp(tall)

    def one(head, _):
        at = lanes_at(head, size)
        dq_ref[:, at], dk_ref[:, at], dv_ref[:, at] = inner_grads(
            q_ref[:, at], k_ref[:, at], v_ref[:, at], dout_ref[:, at], weights_ref[head],
            state_ref[head].astype(half), decay_at(tall, flat_ref, head), column_of(entering, head)
        )

    lax.fori_loop(0, weights_ref.shape[0], one, None)


def shape(dims, kind=flt):
    return jax.ShapeDtypeStruct(dims, kind)


def kernel(body, out_shape, flops, moved, name, placed=True, limit=16, after=None, **more):
    cost = pl.CostEstimate(flops=int(flops), bytes_accessed=int(moved), transcendentals=0)
    settings = dict(
        out_shape=out_shape,
        compiler_params=pltpu.CompilerParams(vmem_limit_bytes=limit << 20),
        cost_estimate=cost,
        name=name,
    )
    settings.update(more)

    def space(place):
        if after is not None and place >= after:
            return pl.ANY
        return pltpu.SMEM if placed and place == 0 else pltpu.VMEM

    return lambda *arrays: pl.pallas_call(
        body,
        in_specs=[pl.BlockSpec(memory_space=space(place)) for place in range(len(arrays))],
        **settings,
    )(*arrays)


def on_device(behaviors, log_decay, qkv_weight, cotangent):
    rows = behaviors[0]
    rates = log_decay[0]
    upstream = cotangent[0]
    length, width = rows.shape
    heads = rates.shape[0]
    size = width // heads
    users = lax.axis_size("batch")
    count = lax.axis_size("seq")
    segments = count // heads
    chips = users // CORES
    pairs = heads // PAIR
    wide = PAIR * size
    at = jnp.stack([lax.axis_index("batch"), lax.axis_index("seq")]).astype(jnp.int32)

    def along_line(array, step):
        pairs_of = [(s, s // heads * heads + (s + step) % heads) for s in range(count)]
        return lax.ppermute(array, "seq", pairs_of)

    def along_segments(array, step):
        return lax.ppermute(array, "seq", [(s, (s + step * heads) % count) for s in range(count)])

    def along_users(array, step, turn):
        pairs_of = [
            (u, (u // CORES + step) % chips * CORES + (u + turn) % CORES) for u in range(users)
        ]
        return lax.ppermute(array, "batch", pairs_of)

    def line_exchange(arrays):
        return [arrays[0]] + [along_line(arrays[step], step) for step in range(1, heads)]

    whole = lambda dims: pl.BlockSpec(dims, lambda i: (0,) * len(dims))
    column = pl.BlockSpec((length, wide), lambda i: (0, i))
    weight_at = lambda part: pl.BlockSpec((width, wide), lambda i: (0, part * pairs + i))
    tokens = lambda kind: shape((length, width), kind)
    state = shape((size, size))
    smem = pl.BlockSpec(memory_space=pltpu.SMEM)
    share = heads * size // count
    slices = shape((count, share, size))
    square = length * length * size

    def exchange(own, other, moved):
        dims = own.shape[1:]
        came = along_users(other, 0, 1)
        both = kernel(
            pair_kernel, [shape((CORES,) + dims)] * chips, 1 << 16, moved, "pair", False
        )(own, came)
        return [both[0]] + [along_users(both[step], step, 0) for step in range(1, chips)]

    q, k, v, tall, flat, sums, top, low, weight_columns = pl.pallas_call(
        functools.partial(project_kernel, size),
        grid=(pairs,),
        in_specs=[smem, whole((length, width)), weight_at(0), weight_at(1), weight_at(2), whole((heads, length))],
        out_specs=[column] * 3 + [whole((length, heads)), whole((heads, length))]
        + [pl.BlockSpec((count // pairs, share + EXTRA, size), lambda i: (i, 0, 0))]
        + [whole((length // 2, width))] * 2 + [whole((width, 3 * size))],
        out_shape=[tokens(half)] * 3 + [shape((length, heads)), shape((heads, length))]
        + [shape((count, share + EXTRA, size))] + [shape((length // 2, width))] * 2
        + [shape((width, 3 * size), half)],
        scratch_shapes=[pltpu.VMEM((length, heads), flt)],
        compiler_params=pltpu.CompilerParams(vmem_limit_bytes=59 << 20),
        cost_estimate=pl.CostEstimate(
            flops=6 * length * width * width, bytes_accessed=8 * width * width, transcendentals=0
        ),
        name="project",
    )(at, rows, qkv_weight, qkv_weight, qkv_weight, rates)
    ahead, astern = (lambda array: along_users(array, 1, 0)), (lambda array: along_users(array, chips - 1, 0))
    top_before, low_behind = ahead(top), astern(low)
    low_before, top_behind = ahead(low), astern(top)
    top_beyond, low_beyond = ahead(top_before), astern(low_behind)
    near_wide = [top, low, top_before, low_before, top_beyond, low_beyond, top_behind, low_behind]
    far_wide = [along_users(array, 0, 1) for array in near_wide]

    def mark_of(*arrays):
        return sum(array[-EXTRA:, :size] for array in arrays)

    got = lax.all_to_all(sums, "seq", 0, 0)
    entered, block_rates = kernel(
        scan_kernel, [slices, shape((count, EXTRA, size))], 1 << 18, 1 << 20, "scan", False
    )(got, mark_of(top_before, low_behind))
    state_in = lax.all_to_all(entered, "seq", 0, 0).reshape(heads, size, size)

    weights, intra = kernel(
        functools.partial(weights_kernel, heads, size),
        [shape((heads, length, length), half), tokens(flt)],
        heads * 4 * square, 5 << 20, "weights", False,
    )(q, k, v, tall, flat)

    mixed, d_output, sums = kernel(
        functools.partial(mix_kernel, size),
        [tokens(half), tokens(half), slices],
        heads * 2 * square, 5 << 20, "mix", False,
    )(q, intra, upstream, tall, state_in, mark_of(low_before, top_behind))
    got = lax.all_to_all(sums, "seq", 0, 0)
    packed = kernel(
        functools.partial(pack_kernel, size),
        [shape((chips, length + size + EXTRA, size))] * CORES, 1 << 18, 3 << 20, "pack",
    )(at, d_output, state_in, rates)
    every = exchange(*packed, 3 << 20)

    def recall(wide, after, name):
        count = len(wide) // 2
        return kernel(
            recall_kernel,
            [shape((count, length, width), half), shape((count, length, 3 * size), half), shape((EXTRA, size))],
            6 * length * width * size * count, 8 << 20, name, False, after=2, limit=50,
            scratch_shapes=[pltpu.VMEM((count, length, width), flt), pltpu.SemaphoreType.DMA((2 * count,))],
        )(weight_columns, after, *wide)

    pieces = {(step, 0): near_wide[2 * step : 2 * step + 2] for step in range(chips)}
    pieces.update({(step, 1): far_wide[2 * step : 2 * step + 2] for step in range(chips)})
    wides = [piece for place in ORDER for piece in pieces[place]]
    first_rows, first_qkv, mark = recall(wides[: 2 * FIRST], mark_of(top_before), "recall")

    entered, mark = kernel(
        back_scan_kernel, [slices, shape((EXTRA, size))], 1 << 18, 1 << 20, "back_scan", False
    )(got, block_rates, mark + mark_of(top_beyond, low_beyond))
    back = lax.all_to_all(entered, "seq", 0, 0).reshape(heads, size, size)
    d_query, key_part, value_part = kernel(
        functools.partial(inner_kernel, size),
        [tokens(half), tokens(flt), tokens(flt)], heads * 10 * square, 6 << 20, "inner", False,
    )(q, k, v, d_output, weights, state_in, tall, flat)
    rest_rows, rest_qkv, mark = recall(wides[2 * FIRST :], mark, "recall_rest")
    *chosen, back_bf = kernel(
        choose_kernel, [shape((chips, size, size))] * CORES + [shape((heads, size, size), half)],
        1 << 18, 1 << 20, "choose",
    )(at, back, mark)
    owned = exchange(*chosen, 1 << 20)

    owner_tall, turned_query, key_inner, value_inner = kernel(
        functools.partial(owner_kernel, size),
        [shape((length, users)), shape((size, users * length), half)] + [shape((users, length, size))] * 2,
        users * 12 * square, 6 << 20, "owner", False,
        scratch_shapes=[pltpu.VMEM((users, length), flt), pltpu.VMEM((users, length + size, size), flt)],
    )(first_qkv, rest_qkv, *every)
    turned = kernel(
        functools.partial(late_kernel, size),
        shape((3 * size, users * length), half), users * 2 * square, 4 << 20, "late", False,
        scratch_shapes=[pltpu.VMEM((users, size, size), half)],
    )(first_qkv, rest_qkv, key_inner, value_inner, owner_tall, turned_query, *owned)

    weight_rows = lambda part: pl.BlockSpec((wide, width), lambda i: (i, part))
    d_rows = pl.pallas_call(
        functools.partial(rows_kernel, size),
        grid=(pairs,),
        in_specs=[whole((length, width))] * 5
        + [whole((heads, size, size)), whole((length, heads))]
        + [weight_rows(part) for part in range(3)],
        out_specs=column,
        out_shape=tokens(half),
        scratch_shapes=[pltpu.VMEM((length, width), half)] * 2,
        compiler_params=pltpu.CompilerParams(vmem_limit_bytes=24 << 20),
        cost_estimate=pl.CostEstimate(
            flops=6 * length * width * width, bytes_accessed=8 * width * width, transcendentals=0
        ),
        name="rows",
    )(d_query, key_part, value_part, k, v, back_bf, tall, qkv_weight, qkv_weight, qkv_weight)
    def term(step):
        return kernel(
            functools.partial(term_kernel, step),
            shape((3 * size, width // segments)),
            6 * users * length * size * width // segments, 3 << 20, "term",
        )(at, turned, first_rows, rest_rows)

    got = [along_segments(term(step), step) for step in (2, 1, 3)] + [term(0)]
    pieces = kernel(
        fold_kernel, [shape((width // count, 3 * size))] * heads, 1 << 20, 2 << 20, "fold",
        scratch_shapes=[pltpu.VMEM((heads, width // count, 3 * size), flt)], after=5,
    )(at, *got, d_rows)
    got = line_exchange(pieces)
    mine = kernel(gather_kernel, shape((width // count, 3 * size)), 1 << 18, 1 << 18, "gather", False)(*got)

    other = along_users(mine, 0, 1)
    both = kernel(both_kernel, shape((CORES, width // count, 3 * size)), 1 << 16, 1 << 17, "both", False)(mine, other)
    summed = [both] + [along_users(both, step, 0) for step in range(1, chips)]
    squares = kernel(square_kernel, shape((count, EXTRA, size)), 1 << 18, 1 << 18, "square", False)(*summed)
    squares = lax.all_to_all(squares, "seq", 0, 0)
    weight_step = kernel(
        step_kernel, shape((width // count, 3 * width)), 1 << 18, 1 << 20, "step",
        scratch_shapes=[pltpu.VMEM((heads, width // count, 3 * size), flt)],
    )(at, squares, *summed)

    return (mixed[None], d_rows[None], weight_step)


def solution(mesh):
    placed = (P("batch", "seq", None), P("batch", None, "seq"), P(), P("batch", "seq", None))
    return jax.shard_map(
        on_device,
        mesh=mesh,
        in_specs=placed,
        out_specs=(P("batch", "seq", None), P("batch", "seq", None), P("seq", None)),
        check_vma=False,
    )
```

```python
import functools

import jax
import jax.numpy as jnp
from jax import lax
from jax.experimental import pallas as pl
from jax.experimental.pallas import tpu as pltpu
from jax.sharding import PartitionSpec as P

epsilon = 1e-06
flt = jnp.float32
half = jnp.bfloat16
PAIR = 2
CORES = 2
EXTRA = 8
ORDER = ((0, 0), (1, 0), (3, 0), (2, 0), (0, 1), (1, 1), (2, 1), (3, 1))
FIRST = 3


def dot(a, b, ca, cb, precision=None):
    return lax.dot_general(
        a, b, (((ca,), (cb,)), ((), ())), preferred_element_type=flt, precision=precision
    )


def ordered(length):
    at = lax.broadcasted_iota(jnp.int32, (length, length), 0)
    source = lax.broadcasted_iota(jnp.int32, (length, length), 1)
    return at >= source


def running(rates):
    ones = ordered(rates.shape[1]).astype(flt)
    exact = lax.Precision.HIGHEST
    return dot(ones, rates, 1, 1, exact), dot(rates, ones, 1, 1, exact)


def decay_within(tall, flat, index):
    length = tall.shape[0]
    causal = ordered(length)
    spread = tall[:, index : index + 1] - flat[index : index + 1, :]
    return jnp.where(causal, jnp.exp(jnp.where(causal, spread, 0.0)), 0.0)


def place_in(index, step, count):
    return lax.rem(index + step + count, count)


def put_sum(sent_ref, lane, total):
    pieces = sent_ref.shape[0] // PAIR
    share = total.shape[0] // pieces
    for piece in range(pieces):
        sent_ref[lane * pieces + piece, :share, :] = total[piece * share : (piece + 1) * share]


def project_kernel(size, at_ref, rows_ref, wq_ref, wk_ref, wv_ref, rates_ref, q_ref, k_ref, v_ref,
                   tall_ref, flat_ref, sent_ref, top_ref, low_ref, own_ref, leaving_ref):
    step = pl.program_id(0)
    rows = rows_ref[...]
    width = top_ref.shape[1] // pl.num_programs(0)
    middle = top_ref.shape[0]
    columns = pl.ds(pl.multiple_of(step * width, width), width)
    top_ref[:, columns] = rows_ref[:middle, columns].astype(flt)
    low_ref[:, columns] = rows_ref[middle:, columns].astype(flt)
    for lane in range(PAIR):

        @pl.when(at_ref[0] == step * PAIR + lane)
        def _():
            for part, weight_ref in enumerate((wq_ref, wk_ref, wv_ref)):
                own_ref[:, part * size : (part + 1) * size] = weight_ref[:, lane * size : (lane + 1) * size]

    @pl.when(step == 0)
    def _():
        tall, flat = running(rates_ref[...])
        tall_ref[...] = tall
        flat_ref[...] = flat
        leaving_ref[...] = jnp.exp(tall[-1:] - tall)

    k = dot(rows, wk_ref[...], 1, 0).astype(half)
    v = dot(rows, wv_ref[...], 1, 0).astype(half)
    k_ref[...] = k
    v_ref[...] = v
    leaving = leaving_ref[...]
    lanes = lax.broadcasted_iota(jnp.int32, leaving.shape, 1)
    pieces = sent_ref.shape[0] // PAIR
    share = sent_ref.shape[1] - EXTRA
    for lane in range(PAIR):
        at = slice(lane * size, (lane + 1) * size)
        head = step * PAIR + lane
        column = jnp.sum(jnp.where(lanes == head, leaving, 0.0), axis=1, keepdims=True)
        keyed = (k[:, at].astype(flt) * column).astype(half)
        put_sum(sent_ref, lane, dot(keyed, v[:, at], 0, 0))
        last = flat_ref[pl.ds(head, 1), :][:, -1:]
        rate = jnp.broadcast_to(jnp.exp(last), (EXTRA, size))
        for piece in range(pieces):
            sent_ref[lane * pieces + piece, share:, :] = rate
    q_ref[...] = dot(rows, wq_ref[...], 1, 0).astype(half)


def scan_kernel(got_ref, mark_ref, out_ref, rates_ref):
    count, share, columns = out_ref.shape
    state = jnp.zeros((share, columns), flt)
    for block in range(count):
        out_ref[block] = state
        rates_ref[block] = got_ref[block, share:, :]
        state = got_ref[block, share : share + 1, :] * state + got_ref[block, :share, :]


def back_scan_kernel(got_ref, rates_ref, after_ref, out_ref, mark_ref):
    count, share, columns = out_ref.shape
    mark_ref[...] = after_ref[...] * 0.0
    state = jnp.zeros((share, columns), flt)
    for block in range(count - 1, -1, -1):
        out_ref[block] = state
        state = rates_ref[block, :1, :] * state + got_ref[block]


def column_of(table, index):
    lanes = lax.broadcasted_iota(jnp.int32, table.shape, 1)
    return jnp.sum(jnp.where(lanes == index, table, 0.0), axis=1, keepdims=True)


def decay_at(tall, flat_ref, index):
    length = tall.shape[0]
    causal = ordered(length)
    spread = column_of(tall, index) - flat_ref[pl.ds(index, 1), :]
    return jnp.where(causal, jnp.exp(jnp.where(causal, spread, 0.0)), 0.0)


def lanes_at(head, size):
    return pl.ds(pl.multiple_of(head * size, size), size)


def weights_kernel(heads, size, q_ref, k_ref, v_ref, tall_ref, flat_ref, weights_ref, intra_ref):
    tall = tall_ref[...]

    def one(head, _):
        at = lanes_at(head, size)
        scores = dot(q_ref[:, at], k_ref[:, at], 1, 1)
        weights = (scores * decay_at(tall, flat_ref, head)).astype(half)
        weights_ref[head] = weights
        intra_ref[:, at] = dot(weights, v_ref[:, at], 1, 0)

    lax.fori_loop(0, heads, one, None)


def mix_kernel(size, q_ref, intra_ref, up_ref, tall_ref, state_ref, after_ref, mixed_ref, dout_ref, sent_ref):
    heads = state_ref.shape[0]
    pieces = sent_ref.shape[0] // heads
    share = size // pieces
    entering = jnp.exp(tall_ref[...])

    def one(head, _):
        at = lanes_at(head, size)
        q = q_ref[:, at]
        column = column_of(entering, head)
        output = intra_ref[:, at] + dot(q, state_ref[head].astype(half), 1, 0) * column
        scale = lax.rsqrt(jnp.mean(output * output, axis=-1, keepdims=True) + epsilon)
        normed = output * scale
        mixed_ref[:, at] = normed.astype(half)
        incoming = up_ref[:, at].astype(flt)
        along = jnp.mean(normed * incoming, axis=-1, keepdims=True)
        d_output = (scale * (incoming - normed * along)).astype(half)
        dout_ref[:, at] = d_output
        lifted = (q.astype(flt) * column).astype(half)
        total = dot(lifted, d_output, 0, 0)
        for piece in range(pieces):
            sent_ref[head * pieces + piece] = total[piece * share : (piece + 1) * share]

    lax.fori_loop(0, heads, one, None, unroll=2)


def head_at(at_ref, step, turn, chips):
    chip, core = at_ref[0] // CORES, lax.rem(at_ref[0], CORES)
    return place_in(chip, step, chips) * CORES + lax.rem(core + turn, CORES)


def pack_kernel(size, at_ref, dout_ref, state_ref, rates_ref, own_ref, other_ref):
    length = dout_ref.shape[0]
    chips = own_ref.shape[0]
    for turn, out_ref in enumerate((own_ref, other_ref)):
        for step in range(chips):
            head = head_at(at_ref, step, turn, chips)
            columns = pl.ds(pl.multiple_of(head * size, size), size)
            out_ref[step, :length, :] = dout_ref[:, columns].astype(flt)
            out_ref[step, length : length + size, :] = state_ref[head]
            row = rates_ref[pl.ds(head, 1), :]
            out_ref[step, length + size :, :] = jnp.zeros((EXTRA, size), flt)
            for part in range(length // size):
                to = length + size + part
                out_ref[step, to : to + 1, :] = row[:, part * size : (part + 1) * size]


def pair_kernel(own_ref, came_ref, *out_refs):
    for step, out_ref in enumerate(out_refs):
        out_ref[0] = own_ref[step]
        out_ref[1] = came_ref[step]


def recall_kernel(weight_ref, after_ref, *refs):
    wide_refs, (rows_ref, qkv_ref, mark_ref, held_ref, sem) = refs[:-5], refs[-5:]
    count, length, _ = rows_ref.shape
    middle = length // 2
    copies = [
        pltpu.make_async_copy(wide_ref, held_ref.at[part // 2, pl.ds(part % 2 * middle, middle)], sem.at[part])
        for part, wide_ref in enumerate(wide_refs)
    ]
    for copy in copies:
        copy.start()
    mark_ref[...] = jnp.zeros(mark_ref.shape, flt)

    def one(place, _):
        for part in range(2):
            target = held_ref.at[place, pl.ds(part * middle, middle)]
            pltpu.make_async_copy(wide_refs[0], target, sem.at[2 * place + part]).wait()
        rows = held_ref[place].astype(half)
        rows_ref[place] = rows
        qkv_ref[place] = dot(rows, weight_ref[...], 1, 0).astype(half)

    lax.fori_loop(0, count, one, None)


def inner_grads(q, k, v, d_output, weights, state, within, entering):
    d_score = (dot(d_output, v, 1, 1) * within).astype(half)
    d_query = dot(d_score, k, 1, 0) + entering * dot(d_output, state, 1, 1)
    return d_query.astype(half), dot(d_score, q, 0, 0), dot(weights, d_output, 0, 0)


def owner_kernel(size, first_ref, rest_ref, *refs):
    got_refs, (tall_ref, turned_ref, dk_ref, dv_ref, flat_held, got_held) = refs[:-6], refs[-6:]
    length = first_ref.shape[1]
    base = length + size
    gots = [got_refs[step].at[turn] for step, turn in ORDER]
    rates = jnp.concatenate(
        [
            jnp.concatenate([got[base + part : base + part + 1, :] for part in range(length // size)], axis=1)
            for got in gots
        ],
        axis=0,
    )
    tall, flat = running(rates)
    tall_ref[...] = tall
    flat_held[...] = flat
    for place, got in enumerate(gots):
        got_held[place] = got[:base, :]
    entering = jnp.exp(tall)

    def one(place, qkv):
        q, k, v = (qkv[:, part * size : (part + 1) * size] for part in range(3))
        within = decay_at(tall, flat_held, place)
        weights = (dot(q, k, 1, 1) * within).astype(half)
        d_output = got_held[place, :length, :].astype(half)
        state = got_held[place, length:, :].astype(half)
        d_query, dk_ref[place], dv_ref[place] = inner_grads(
            q, k, v, d_output, weights, state, within, column_of(entering, place)
        )
        turned_ref[:, lanes_at(place, length)] = d_query.T

    lax.fori_loop(0, FIRST, lambda place, _: one(place, first_ref[place]), None)
    lax.fori_loop(FIRST, len(ORDER), lambda place, _: one(place, rest_ref[place - FIRST]), None)


def late_kernel(size, first_ref, rest_ref, dk_ref, dv_ref, tall_ref, dq_ref, *refs):
    refs[-2][:size, :] = dq_ref[...]
    back_refs, (out_ref, held_ref) = refs[:-2], refs[-2:]
    length = first_ref.shape[1]
    tall = tall_ref[...]
    leaving = jnp.exp(tall[-1:] - tall)
    for place, (step, turn) in enumerate(ORDER):
        held_ref[place] = back_refs[step][turn].astype(half)

    def one(place, k, v):
        column = column_of(leaving, place)
        back = held_ref[place]
        d_key = (dk_ref[place] + column * dot(v, back, 1, 1)).astype(half)
        d_value = (dv_ref[place] + column * dot(k, back, 1, 0)).astype(half)
        out_ref[size : 2 * size, lanes_at(place, length)] = d_key.T
        out_ref[2 * size :, lanes_at(place, length)] = d_value.T

    def near(place, _):
        one(place, first_ref[place, :, size : 2 * size], first_ref[place, :, 2 * size :])

    def far(place, _):
        at = place - FIRST
        one(place, rest_ref[at, :, size : 2 * size], rest_ref[at, :, 2 * size :])

    lax.fori_loop(0, FIRST, near, None)
    lax.fori_loop(FIRST, len(ORDER), far, None)


def choose_kernel(at_ref, back_ref, after_ref, own_ref, other_ref, keep_ref):
    chips = own_ref.shape[0]
    for step in range(chips):
        own_ref[step] = back_ref[head_at(at_ref, step, 0, chips)]
        other_ref[step] = back_ref[head_at(at_ref, step, 1, chips)]
    keep_ref[...] = back_ref[...].astype(half)


def term_kernel(step, at_ref, turned_ref, first_ref, rest_ref, out_ref):
    _, length, width = first_ref.shape
    users = len(ORDER)
    share = out_ref.shape[1]
    target = place_in(at_ref[1] // users, step, width // share)
    columns = pl.ds(pl.multiple_of(target * share, share), share)
    middle = FIRST * length
    first = first_ref[:, :, columns].reshape(middle, share)
    rest = rest_ref[:, :, columns].reshape(users * length - middle, share)
    out_ref[...] = dot(turned_ref[:, :middle], first, 1, 0) + dot(turned_ref[:, middle:], rest, 1, 0)


def fold_kernel(at_ref, *refs):
    got_refs, out_refs, slots_ref = refs[:4], refs[5:-1], refs[-1]
    blocks = len(out_refs)
    total = got_refs[0][...]
    for got_ref in got_refs[1:]:
        total += got_ref[...]
    turned = total.T
    line = lax.rem(at_ref[1], blocks)
    share = turned.shape[0] // blocks
    for block in range(blocks):
        slots_ref[block] = turned[block * share : (block + 1) * share]
    for step, out_ref in enumerate(out_refs):
        out_ref[...] = slots_ref[place_in(line, step, blocks)]


def gather_kernel(*refs):
    total = refs[0][...]
    for got_ref in refs[1:-1]:
        total += got_ref[...]
    refs[-1][...] = total


def both_kernel(mine_ref, other_ref, out_ref):
    out_ref[0] = mine_ref[...]
    out_ref[1] = other_ref[...]


def square_kernel(*refs):
    got_refs, out_ref = refs[:-1], refs[-1]
    size = out_ref.shape[2]
    for part in range(3):
        total = jnp.zeros((1, size), flt)
        for got_ref in got_refs:
            for core in range(CORES):
                piece = got_ref[core, :, part * size : (part + 1) * size]
                total += jnp.sum(piece * piece, axis=0, keepdims=True)
        out_ref[:, part : part + 1, :] = jnp.broadcast_to(total[None], (out_ref.shape[0], 1, size))
    out_ref[:, 3:, :] = jnp.zeros((out_ref.shape[0], EXTRA - 3, size), flt)


def step_kernel(at_ref, squares_ref, *refs):
    got_refs, out_ref, slots_ref = refs[:-2], refs[-2], refs[-1]
    heads, share, width = slots_ref.shape
    size = width // 3
    chips = heads // CORES
    chip, core = at_ref[0] // CORES, lax.rem(at_ref[0], CORES)
    for step, got_ref in enumerate(got_refs):
        for turn in range(CORES):
            head = place_in(chip, -step, chips) * CORES + lax.rem(core + turn, CORES)
            slots_ref[head] = got_ref[turn]
    total = jnp.sum(squares_ref[...], axis=0)
    entries = float(heads * size) ** 2
    for part in range(3):
        mean = jnp.sum(total[part : part + 1], axis=1, keepdims=True) / entries
        factor = lax.rsqrt(mean + epsilon)
        for head in range(heads):
            at = (part * heads + head) * size
            out_ref[:, at : at + size] = slots_ref[head, :, part * size : (part + 1) * size] * factor


def rows_kernel(size, dq_ref, dki_ref, dvi_ref, k_ref, v_ref, back_ref, tall_ref,
                wq_ref, wk_ref, wv_ref, out_ref, dk_ref, dv_ref):
    @pl.when(pl.program_id(0) == 0)
    def _():
        tall = tall_ref[...]
        leaving = jnp.exp(tall[-1:] - tall)
        for head in range(back_ref.shape[0]):
            at = slice(head * size, (head + 1) * size)
            column = leaving[:, head : head + 1]
            back = back_ref[head]
            dk_ref[:, at] = (dki_ref[:, at] + column * dot(v_ref[:, at], back, 1, 1)).astype(half)
            dv_ref[:, at] = (dvi_ref[:, at] + column * dot(k_ref[:, at], back, 1, 0)).astype(half)

    total = dot(dq_ref[...], wq_ref[...], 1, 1)
    total += dot(dk_ref[...], wk_ref[...], 1, 1)
    total += dot(dv_ref[...], wv_ref[...], 1, 1)
    out_ref[...] = total.astype(half)


def inner_kernel(size, q_ref, k_ref, v_ref, dout_ref, weights_ref, state_ref, tall_ref, flat_ref,
                 dq_ref, dk_ref, dv_ref):
    tall = tall_ref[...]
    entering = jnp.exp(tall)

    def one(head, _):
        at = lanes_at(head, size)
        dq_ref[:, at], dk_ref[:, at], dv_ref[:, at] = inner_grads(
            q_ref[:, at], k_ref[:, at], v_ref[:, at], dout_ref[:, at], weights_ref[head],
            state_ref[head].astype(half), decay_at(tall, flat_ref, head), column_of(entering, head)
        )

    lax.fori_loop(0, weights_ref.shape[0], one, None)


def shape(dims, kind=flt):
    return jax.ShapeDtypeStruct(dims, kind)


def kernel(body, out_shape, flops, moved, name, placed=True, limit=16, after=None, **more):
    cost = pl.CostEstimate(flops=int(flops), bytes_accessed=int(moved), transcendentals=0)
    settings = dict(
        out_shape=out_shape,
        compiler_params=pltpu.CompilerParams(vmem_limit_bytes=limit << 20),
        cost_estimate=cost,
        name=name,
    )
    settings.update(more)

    def space(place):
        if after is not None and place >= after:
            return pl.ANY
        return pltpu.SMEM if placed and place == 0 else pltpu.VMEM

    return lambda *arrays: pl.pallas_call(
        body,
        in_specs=[pl.BlockSpec(memory_space=space(place)) for place in range(len(arrays))],
        **settings,
    )(*arrays)


def on_device(behaviors, log_decay, qkv_weight, cotangent):
    rows = behaviors[0]
    rates = log_decay[0]
    upstream = cotangent[0]
    length, width = rows.shape
    heads = rates.shape[0]
    size = width // heads
    users = lax.axis_size("batch")
    count = lax.axis_size("seq")
    segments = count // heads
    chips = users // CORES
    pairs = heads // PAIR
    wide = PAIR * size
    at = jnp.stack([lax.axis_index("batch"), lax.axis_index("seq")]).astype(jnp.int32)

    def along_line(array, step):
        pairs_of = [(s, s // heads * heads + (s + step) % heads) for s in range(count)]
        return lax.ppermute(array, "seq", pairs_of)

    def along_segments(array, step):
        return lax.ppermute(array, "seq", [(s, (s + step * heads) % count) for s in range(count)])

    def along_users(array, step, turn):
        pairs_of = [
            (u, (u // CORES + step) % chips * CORES + (u + turn) % CORES) for u in range(users)
        ]
        return lax.ppermute(array, "batch", pairs_of)

    def line_exchange(arrays):
        return [arrays[0]] + [along_line(arrays[step], step) for step in range(1, heads)]

    whole = lambda dims: pl.BlockSpec(dims, lambda i: (0,) * len(dims))
    column = pl.BlockSpec((length, wide), lambda i: (0, i))
    weight_at = lambda part: pl.BlockSpec((width, wide), lambda i: (0, part * pairs + i))
    tokens = lambda kind: shape((length, width), kind)
    state = shape((size, size))
    smem = pl.BlockSpec(memory_space=pltpu.SMEM)
    share = heads * size // count
    slices = shape((count, share, size))
    square = length * length * size

    def exchange(own, other, moved):
        dims = own.shape[1:]
        came = along_users(other, 0, 1)
        both = kernel(
            pair_kernel, [shape((CORES,) + dims)] * chips, 1 << 16, moved, "pair", False
        )(own, came)
        return [both[0]] + [along_users(both[step], step, 0) for step in range(1, chips)]

    q, k, v, tall, flat, sums, top, low, weight_columns = pl.pallas_call(
        functools.partial(project_kernel, size),
        grid=(pairs,),
        in_specs=[smem, whole((length, width)), weight_at(0), weight_at(1), weight_at(2), whole((heads, length))],
        out_specs=[column] * 3 + [whole((length, heads)), whole((heads, length))]
        + [pl.BlockSpec((count // pairs, share + EXTRA, size), lambda i: (i, 0, 0))]
        + [whole((length // 2, width))] * 2 + [whole((width, 3 * size))],
        out_shape=[tokens(half)] * 3 + [shape((length, heads)), shape((heads, length))]
        + [shape((count, share + EXTRA, size))] + [shape((length // 2, width))] * 2
        + [shape((width, 3 * size), half)],
        scratch_shapes=[pltpu.VMEM((length, heads), flt)],
        compiler_params=pltpu.CompilerParams(vmem_limit_bytes=59 << 20),
        cost_estimate=pl.CostEstimate(
            flops=6 * length * width * width, bytes_accessed=8 * width * width, transcendentals=0
        ),
        name="project",
    )(at, rows, qkv_weight, qkv_weight, qkv_weight, rates)
    ahead, astern = (lambda array: along_users(array, 1, 0)), (lambda array: along_users(array, chips - 1, 0))
    top_before, low_behind = ahead(top), astern(low)
    low_before, top_behind = ahead(low), astern(top)
    top_beyond, low_beyond = ahead(top_before), astern(low_behind)
    near_wide = [top, low, top_before, low_before, top_beyond, low_beyond, top_behind, low_behind]
    far_wide = [along_users(array, 0, 1) for array in near_wide]

    def mark_of(*arrays):
        return sum(array[-EXTRA:, :size] for array in arrays)

    got = lax.all_to_all(sums, "seq", 0, 0)
    entered, block_rates = kernel(
        scan_kernel, [slices, shape((count, EXTRA, size))], 1 << 18, 1 << 20, "scan", False
    )(got, mark_of(top_before, low_behind))
    state_in = lax.all_to_all(entered, "seq", 0, 0).reshape(heads, size, size)

    weights, intra = kernel(
        functools.partial(weights_kernel, heads, size),
        [shape((heads, length, length), half), tokens(flt)],
        heads * 4 * square, 5 << 20, "weights", False,
    )(q, k, v, tall, flat)

    mixed, d_output, sums = kernel(
        functools.partial(mix_kernel, size),
        [tokens(half), tokens(half), slices],
        heads * 2 * square, 5 << 20, "mix", False,
    )(q, intra, upstream, tall, state_in, mark_of(low_before, top_behind))
    got = lax.all_to_all(sums, "seq", 0, 0)
    packed = kernel(
        functools.partial(pack_kernel, size),
        [shape((chips, length + size + EXTRA, size))] * CORES, 1 << 18, 3 << 20, "pack",
    )(at, d_output, state_in, rates)
    every = exchange(*packed, 3 << 20)

    def recall(wide, after, name):
        count = len(wide) // 2
        return kernel(
            recall_kernel,
            [shape((count, length, width), half), shape((count, length, 3 * size), half), shape((EXTRA, size))],
            6 * length * width * size * count, 8 << 20, name, False, after=2, limit=58,
            scratch_shapes=[pltpu.VMEM((count, length, width), flt), pltpu.SemaphoreType.DMA((2 * count,))],
        )(weight_columns, after, *wide)

    pieces = {(step, 0): near_wide[2 * step : 2 * step + 2] for step in range(chips)}
    pieces.update({(step, 1): far_wide[2 * step : 2 * step + 2] for step in range(chips)})
    wides = [piece for place in ORDER for piece in pieces[place]]
    first_rows, first_qkv, mark = recall(wides[: 2 * FIRST], mark_of(top_before), "recall")

    entered, mark = kernel(
        back_scan_kernel, [slices, shape((EXTRA, size))], 1 << 18, 1 << 20, "back_scan", False
    )(got, block_rates, mark + mark_of(top_beyond, low_beyond))
    back = lax.all_to_all(entered, "seq", 0, 0).reshape(heads, size, size)
    d_query, key_part, value_part = kernel(
        functools.partial(inner_kernel, size),
        [tokens(half), tokens(flt), tokens(flt)], heads * 10 * square, 6 << 20, "inner", False,
    )(q, k, v, d_output, weights, state_in, tall, flat)
    rest_rows, rest_qkv, mark = recall(wides[2 * FIRST :], mark, "recall_rest")
    *chosen, back_bf = kernel(
        choose_kernel, [shape((chips, size, size))] * CORES + [shape((heads, size, size), half)],
        1 << 18, 1 << 20, "choose",
    )(at, back, mark)
    owned = exchange(*chosen, 1 << 20)

    owner_tall, turned_query, key_inner, value_inner = kernel(
        functools.partial(owner_kernel, size),
        [shape((length, users)), shape((size, users * length), half)] + [shape((users, length, size))] * 2,
        users * 12 * square, 6 << 20, "owner", False,
        scratch_shapes=[pltpu.VMEM((users, length), flt), pltpu.VMEM((users, length + size, size), flt)],
    )(first_qkv, rest_qkv, *every)
    turned = kernel(
        functools.partial(late_kernel, size),
        shape((3 * size, users * length), half), users * 2 * square, 4 << 20, "late", False,
        scratch_shapes=[pltpu.VMEM((users, size, size), half)],
    )(first_qkv, rest_qkv, key_inner, value_inner, owner_tall, turned_query, *owned)

    weight_rows = lambda part: pl.BlockSpec((wide, width), lambda i: (i, part))
    d_rows = pl.pallas_call(
        functools.partial(rows_kernel, size),
        grid=(pairs,),
        in_specs=[whole((length, width))] * 5
        + [whole((heads, size, size)), whole((length, heads))]
        + [weight_rows(part) for part in range(3)],
        out_specs=column,
        out_shape=tokens(half),
        scratch_shapes=[pltpu.VMEM((length, width), half)] * 2,
        compiler_params=pltpu.CompilerParams(vmem_limit_bytes=24 << 20),
        cost_estimate=pl.CostEstimate(
            flops=6 * length * width * width, bytes_accessed=8 * width * width, transcendentals=0
        ),
        name="rows",
    )(d_query, key_part, value_part, k, v, back_bf, tall, qkv_weight, qkv_weight, qkv_weight)
    def term(step):
        return kernel(
            functools.partial(term_kernel, step),
            shape((3 * size, width // segments)),
            6 * users * length * size * width // segments, 3 << 20, "term",
        )(at, turned, first_rows, rest_rows)

    got = [along_segments(term(step), step) for step in (2, 1, 3)] + [term(0)]
    pieces = kernel(
        fold_kernel, [shape((width // count, 3 * size))] * heads, 1 << 20, 2 << 20, "fold",
        scratch_shapes=[pltpu.VMEM((heads, width // count, 3 * size), flt)], after=5,
    )(at, *got, d_rows)
    got = line_exchange(pieces)
    mine = kernel(gather_kernel, shape((width // count, 3 * size)), 1 << 18, 1 << 18, "gather", False)(*got)

    other = along_users(mine, 0, 1)
    both = kernel(both_kernel, shape((CORES, width // count, 3 * size)), 1 << 16, 1 << 17, "both", False)(mine, other)
    summed = [both] + [along_users(both, step, 0) for step in range(1, chips)]
    squares = kernel(square_kernel, shape((count, EXTRA, size)), 1 << 18, 1 << 18, "square", False)(*summed)
    squares = lax.all_to_all(squares, "seq", 0, 0)
    weight_step = kernel(
        step_kernel, shape((width // count, 3 * width)), 1 << 18, 1 << 20, "step",
        scratch_shapes=[pltpu.VMEM((heads, width // count, 3 * size), flt)],
    )(at, squares, *summed)

    return (mixed[None], d_rows[None], weight_step)


def solution(mesh):
    placed = (P("batch", "seq", None), P("batch", None, "seq"), P(), P("batch", "seq", None))
    return jax.shard_map(
        on_device,
        mesh=mesh,
        in_specs=placed,
        out_specs=(P("batch", "seq", None), P("batch", "seq", None), P("seq", None)),
        check_vma=False,
    )
```

```python
import functools

import jax
import jax.numpy as jnp
from jax import lax
from jax.experimental import pallas as pl
from jax.experimental.pallas import tpu as pltpu
from jax.sharding import PartitionSpec as P

epsilon = 1e-06
flt = jnp.float32
half = jnp.bfloat16
PAIR = 2
CORES = 2
EXTRA = 8
ORDER = ((0, 0), (1, 0), (3, 0), (2, 0), (0, 1), (1, 1), (2, 1), (3, 1))
FIRST = 3


def dot(a, b, ca, cb, precision=None):
    return lax.dot_general(
        a, b, (((ca,), (cb,)), ((), ())), preferred_element_type=flt, precision=precision
    )


def ordered(length):
    at = lax.broadcasted_iota(jnp.int32, (length, length), 0)
    source = lax.broadcasted_iota(jnp.int32, (length, length), 1)
    return at >= source


def running(rates):
    ones = ordered(rates.shape[1]).astype(flt)
    exact = lax.Precision.HIGHEST
    return dot(ones, rates, 1, 1, exact), dot(rates, ones, 1, 1, exact)


def decay_within(tall, flat, index):
    length = tall.shape[0]
    causal = ordered(length)
    spread = tall[:, index : index + 1] - flat[index : index + 1, :]
    return jnp.where(causal, jnp.exp(jnp.where(causal, spread, 0.0)), 0.0)


def place_in(index, step, count):
    return lax.rem(index + step + count, count)


def put_sum(sent_ref, lane, total):
    pieces = sent_ref.shape[0] // PAIR
    share = total.shape[0] // pieces
    for piece in range(pieces):
        sent_ref[lane * pieces + piece, :share, :] = total[piece * share : (piece + 1) * share]


def project_kernel(size, at_ref, rows_ref, wq_ref, wk_ref, wv_ref, rates_ref, q_ref, k_ref, v_ref,
                   tall_ref, flat_ref, sent_ref, top_ref, low_ref, own_ref, leaving_ref):
    step = pl.program_id(0)
    rows = rows_ref[...]
    width = top_ref.shape[1] // pl.num_programs(0)
    middle = top_ref.shape[0]
    columns = pl.ds(pl.multiple_of(step * width, width), width)
    top_ref[:, columns] = rows_ref[:middle, columns].astype(flt)
    low_ref[:, columns] = rows_ref[middle:, columns].astype(flt)
    for lane in range(PAIR):

        @pl.when(at_ref[0] == step * PAIR + lane)
        def _():
            for part, weight_ref in enumerate((wq_ref, wk_ref, wv_ref)):
                own_ref[:, part * size : (part + 1) * size] = weight_ref[:, lane * size : (lane + 1) * size]

    @pl.when(step == 0)
    def _():
        tall, flat = running(rates_ref[...])
        tall_ref[...] = tall
        flat_ref[...] = flat
        leaving_ref[...] = jnp.exp(tall[-1:] - tall)

    k = dot(rows, wk_ref[...], 1, 0).astype(half)
    v = dot(rows, wv_ref[...], 1, 0).astype(half)
    k_ref[...] = k
    v_ref[...] = v
    leaving = leaving_ref[...]
    lanes = lax.broadcasted_iota(jnp.int32, leaving.shape, 1)
    pieces = sent_ref.shape[0] // PAIR
    share = sent_ref.shape[1] - EXTRA
    for lane in range(PAIR):
        at = slice(lane * size, (lane + 1) * size)
        head = step * PAIR + lane
        column = jnp.sum(jnp.where(lanes == head, leaving, 0.0), axis=1, keepdims=True)
        keyed = (k[:, at].astype(flt) * column).astype(half)
        put_sum(sent_ref, lane, dot(keyed, v[:, at], 0, 0))
        last = flat_ref[pl.ds(head, 1), :][:, -1:]
        rate = jnp.broadcast_to(jnp.exp(last), (EXTRA, size))
        for piece in range(pieces):
            sent_ref[lane * pieces + piece, share:, :] = rate
    q_ref[...] = dot(rows, wq_ref[...], 1, 0).astype(half)


def scan_kernel(got_ref, mark_ref, out_ref, rates_ref):
    count, share, columns = out_ref.shape
    state = jnp.zeros((share, columns), flt)
    for block in range(count):
        out_ref[block] = state
        rates_ref[block] = got_ref[block, share:, :]
        state = got_ref[block, share : share + 1, :] * state + got_ref[block, :share, :]


def back_scan_kernel(got_ref, rates_ref, after_ref, out_ref, mark_ref):
    count, share, columns = out_ref.shape
    mark_ref[...] = after_ref[...] * 0.0
    state = jnp.zeros((share, columns), flt)
    for block in range(count - 1, -1, -1):
        out_ref[block] = state
        state = rates_ref[block, :1, :] * state + got_ref[block]


def column_of(table, index):
    lanes = lax.broadcasted_iota(jnp.int32, table.shape, 1)
    return jnp.sum(jnp.where(lanes == index, table, 0.0), axis=1, keepdims=True)


def decay_at(column, flat_ref, index):
    length = column.shape[0]
    causal = ordered(length)
    spread = column - flat_ref[pl.ds(index, 1), :]
    return jnp.where(causal, jnp.exp(jnp.where(causal, spread, 0.0)), 0.0)


def lanes_at(head, size):
    return pl.ds(pl.multiple_of(head * size, size), size)


def weights_kernel(heads, size, q_ref, k_ref, v_ref, tall_ref, flat_ref, weights_ref, intra_ref):
    tall = tall_ref[...]

    def one(head, _):
        at = lanes_at(head, size)
        scores = dot(q_ref[:, at], k_ref[:, at], 1, 1)
        weights = (scores * decay_at(column_of(tall, head), flat_ref, head)).astype(half)
        weights_ref[head] = weights
        intra_ref[:, at] = dot(weights, v_ref[:, at], 1, 0)

    lax.fori_loop(0, heads, one, None)


def mix_kernel(size, q_ref, intra_ref, up_ref, tall_ref, state_ref, after_ref, mixed_ref, dout_ref, sent_ref):
    heads = state_ref.shape[0]
    pieces = sent_ref.shape[0] // heads
    share = size // pieces
    entering = jnp.exp(tall_ref[...])

    def one(head, _):
        at = lanes_at(head, size)
        q = q_ref[:, at]
        column = column_of(entering, head)
        output = intra_ref[:, at] + dot(q, state_ref[head].astype(half), 1, 0) * column
        scale = lax.rsqrt(jnp.mean(output * output, axis=-1, keepdims=True) + epsilon)
        normed = output * scale
        mixed_ref[:, at] = normed.astype(half)
        incoming = up_ref[:, at].astype(flt)
        along = jnp.mean(normed * incoming, axis=-1, keepdims=True)
        d_output = (scale * (incoming - normed * along)).astype(half)
        dout_ref[:, at] = d_output
        lifted = (q.astype(flt) * column).astype(half)
        total = dot(lifted, d_output, 0, 0)
        for piece in range(pieces):
            sent_ref[head * pieces + piece] = total[piece * share : (piece + 1) * share]

    lax.fori_loop(0, heads, one, None, unroll=2)


def head_at(at_ref, step, turn, chips):
    chip, core = at_ref[0] // CORES, lax.rem(at_ref[0], CORES)
    return place_in(chip, step, chips) * CORES + lax.rem(core + turn, CORES)


def pack_kernel(size, at_ref, dout_ref, state_ref, rates_ref, own_ref, other_ref):
    length = dout_ref.shape[0]
    chips = own_ref.shape[0]
    for turn, out_ref in enumerate((own_ref, other_ref)):
        for step in range(chips):
            head = head_at(at_ref, step, turn, chips)
            columns = pl.ds(pl.multiple_of(head * size, size), size)
            out_ref[step, :length, :] = dout_ref[:, columns].astype(flt)
            out_ref[step, length : length + size, :] = state_ref[head]
            row = rates_ref[pl.ds(head, 1), :]
            out_ref[step, length + size :, :] = jnp.zeros((EXTRA, size), flt)
            for part in range(length // size):
                to = length + size + part
                out_ref[step, to : to + 1, :] = row[:, part * size : (part + 1) * size]


def pair_kernel(own_ref, came_ref, *out_refs):
    for step, out_ref in enumerate(out_refs):
        out_ref[0] = own_ref[step]
        out_ref[1] = came_ref[step]


def recall_kernel(weight_ref, after_ref, *refs):
    wide_refs, (rows_ref, qkv_ref, mark_ref, held_ref, sem) = refs[:-5], refs[-5:]
    count, length, _ = rows_ref.shape
    middle = length // 2
    copies = [
        pltpu.make_async_copy(wide_ref, held_ref.at[part // 2, pl.ds(part % 2 * middle, middle)], sem.at[part])
        for part, wide_ref in enumerate(wide_refs)
    ]
    for copy in copies:
        copy.start()
    mark_ref[...] = jnp.zeros(mark_ref.shape, flt)

    def one(place, _):
        for part in range(2):
            target = held_ref.at[place, pl.ds(part * middle, middle)]
            pltpu.make_async_copy(wide_refs[0], target, sem.at[2 * place + part]).wait()
        rows = held_ref[place].astype(half)
        rows_ref[place] = rows
        qkv_ref[place] = dot(rows, weight_ref[...], 1, 0).astype(half)

    lax.fori_loop(0, count, one, None)


def inner_grads(q, k, v, d_output, weights, state, within, entering):
    d_score = (dot(d_output, v, 1, 1) * within).astype(half)
    d_query = dot(d_score, k, 1, 0) + entering * dot(d_output, state, 1, 1)
    return d_query.astype(half), dot(d_score, q, 0, 0), dot(weights, d_output, 0, 0)


def owner_kernel(size, first_ref, rest_ref, *refs):
    got_refs, (tall_ref, turned_ref, dk_ref, dv_ref, flat_held, got_held) = refs[:-6], refs[-6:]
    length = first_ref.shape[1]
    base = length + size
    gots = [got_refs[step].at[turn] for step, turn in ORDER]
    rates = jnp.concatenate(
        [
            jnp.concatenate([got[base + part : base + part + 1, :] for part in range(length // size)], axis=1)
            for got in gots
        ],
        axis=0,
    )
    tall, flat = running(rates)
    tall_ref[...] = tall
    flat_held[...] = flat
    for place, got in enumerate(gots):
        got_held[place] = got[:base, :]

    def one(place, qkv):
        q, k, v = (qkv[:, part * size : (part + 1) * size] for part in range(3))
        column = column_of(tall, place)
        within = decay_at(column, flat_held, place)
        weights = (dot(q, k, 1, 1) * within).astype(half)
        d_output = got_held[place, :length, :].astype(half)
        state = got_held[place, length:, :].astype(half)
        d_query, dk_ref[place], dv_ref[place] = inner_grads(
            q, k, v, d_output, weights, state, within, jnp.exp(column)
        )
        turned_ref[:, lanes_at(place, length)] = d_query.T

    lax.fori_loop(0, FIRST, lambda place, _: one(place, first_ref[place]), None)
    lax.fori_loop(FIRST, len(ORDER), lambda place, _: one(place, rest_ref[place - FIRST]), None)


def late_kernel(size, first_ref, rest_ref, dk_ref, dv_ref, tall_ref, dq_ref, *refs):
    refs[-2][:size, :] = dq_ref[...]
    back_refs, (out_ref, held_ref) = refs[:-2], refs[-2:]
    length = first_ref.shape[1]
    tall = tall_ref[...]
    leaving = jnp.exp(tall[-1:] - tall)
    for place, (step, turn) in enumerate(ORDER):
        held_ref[place] = back_refs[step][turn].astype(half)

    def one(place, k, v):
        column = column_of(leaving, place)
        back = held_ref[place]
        d_key = (dk_ref[place] + column * dot(v, back, 1, 1)).astype(half)
        d_value = (dv_ref[place] + column * dot(k, back, 1, 0)).astype(half)
        out_ref[size : 2 * size, lanes_at(place, length)] = d_key.T
        out_ref[2 * size :, lanes_at(place, length)] = d_value.T

    def near(place, _):
        one(place, first_ref[place, :, size : 2 * size], first_ref[place, :, 2 * size :])

    def far(place, _):
        at = place - FIRST
        one(place, rest_ref[at, :, size : 2 * size], rest_ref[at, :, 2 * size :])

    lax.fori_loop(0, FIRST, near, None)
    lax.fori_loop(FIRST, len(ORDER), far, None)


def choose_kernel(at_ref, back_ref, after_ref, own_ref, other_ref, keep_ref):
    chips = own_ref.shape[0]
    for step in range(chips):
        own_ref[step] = back_ref[head_at(at_ref, step, 0, chips)]
        other_ref[step] = back_ref[head_at(at_ref, step, 1, chips)]
    keep_ref[...] = back_ref[...].astype(half)


def term_kernel(step, at_ref, turned_ref, first_ref, rest_ref, out_ref):
    _, length, width = first_ref.shape
    users = len(ORDER)
    share = out_ref.shape[1]
    target = place_in(at_ref[1] // users, step, width // share)
    columns = pl.ds(pl.multiple_of(target * share, share), share)
    middle = FIRST * length
    first = first_ref[:, :, columns].reshape(middle, share)
    rest = rest_ref[:, :, columns].reshape(users * length - middle, share)
    out_ref[...] = dot(turned_ref[:, :middle], first, 1, 0) + dot(turned_ref[:, middle:], rest, 1, 0)


def fold_kernel(at_ref, *refs):
    got_refs, out_refs, slots_ref = refs[:4], refs[5:-1], refs[-1]
    blocks = len(out_refs)
    total = got_refs[0][...]
    for got_ref in got_refs[1:]:
        total += got_ref[...]
    turned = total.T
    line = lax.rem(at_ref[1], blocks)
    share = turned.shape[0] // blocks
    for block in range(blocks):
        slots_ref[block] = turned[block * share : (block + 1) * share]
    for step, out_ref in enumerate(out_refs):
        out_ref[...] = slots_ref[place_in(line, step, blocks)]


def gather_kernel(*refs):
    total = refs[0][...]
    for got_ref in refs[1:-1]:
        total += got_ref[...]
    refs[-1][...] = total


def both_kernel(mine_ref, other_ref, out_ref):
    out_ref[0] = mine_ref[...]
    out_ref[1] = other_ref[...]


def square_kernel(*refs):
    got_refs, out_ref = refs[:-1], refs[-1]
    size = out_ref.shape[2]
    for part in range(3):
        total = jnp.zeros((1, size), flt)
        for got_ref in got_refs:
            for core in range(CORES):
                piece = got_ref[core, :, part * size : (part + 1) * size]
                total += jnp.sum(piece * piece, axis=0, keepdims=True)
        out_ref[:, part : part + 1, :] = jnp.broadcast_to(total[None], (out_ref.shape[0], 1, size))
    out_ref[:, 3:, :] = jnp.zeros((out_ref.shape[0], EXTRA - 3, size), flt)


def step_kernel(at_ref, squares_ref, *refs):
    got_refs, out_ref, slots_ref = refs[:-2], refs[-2], refs[-1]
    heads, share, width = slots_ref.shape
    size = width // 3
    chips = heads // CORES
    chip, core = at_ref[0] // CORES, lax.rem(at_ref[0], CORES)
    for step, got_ref in enumerate(got_refs):
        for turn in range(CORES):
            head = place_in(chip, -step, chips) * CORES + lax.rem(core + turn, CORES)
            slots_ref[head] = got_ref[turn]
    total = jnp.sum(squares_ref[...], axis=0)
    entries = float(heads * size) ** 2
    for part in range(3):
        mean = jnp.sum(total[part : part + 1], axis=1, keepdims=True) / entries
        factor = lax.rsqrt(mean + epsilon)
        for head in range(heads):
            at = (part * heads + head) * size
            out_ref[:, at : at + size] = slots_ref[head, :, part * size : (part + 1) * size] * factor


def rows_kernel(size, dq_ref, dki_ref, dvi_ref, k_ref, v_ref, back_ref, tall_ref,
                wq_ref, wk_ref, wv_ref, out_ref, dk_ref, dv_ref):
    @pl.when(pl.program_id(0) == 0)
    def _():
        tall = tall_ref[...]
        leaving = jnp.exp(tall[-1:] - tall)
        for head in range(back_ref.shape[0]):
            at = slice(head * size, (head + 1) * size)
            column = leaving[:, head : head + 1]
            back = back_ref[head]
            dk_ref[:, at] = (dki_ref[:, at] + column * dot(v_ref[:, at], back, 1, 1)).astype(half)
            dv_ref[:, at] = (dvi_ref[:, at] + column * dot(k_ref[:, at], back, 1, 0)).astype(half)

    total = dot(dq_ref[...], wq_ref[...], 1, 1)
    total += dot(dk_ref[...], wk_ref[...], 1, 1)
    total += dot(dv_ref[...], wv_ref[...], 1, 1)
    out_ref[...] = total.astype(half)


def inner_kernel(size, q_ref, k_ref, v_ref, dout_ref, weights_ref, state_ref, tall_ref, flat_ref,
                 dq_ref, dk_ref, dv_ref):
    tall = tall_ref[...]

    def one(head, _):
        at = lanes_at(head, size)
        column = column_of(tall, head)
        dq_ref[:, at], dk_ref[:, at], dv_ref[:, at] = inner_grads(
            q_ref[:, at], k_ref[:, at], v_ref[:, at], dout_ref[:, at], weights_ref[head],
            state_ref[head].astype(half), decay_at(column, flat_ref, head), jnp.exp(column)
        )

    lax.fori_loop(0, weights_ref.shape[0], one, None)


def shape(dims, kind=flt):
    return jax.ShapeDtypeStruct(dims, kind)


def kernel(body, out_shape, flops, moved, name, placed=True, limit=16, after=None, **more):
    cost = pl.CostEstimate(flops=int(flops), bytes_accessed=int(moved), transcendentals=0)
    settings = dict(
        out_shape=out_shape,
        compiler_params=pltpu.CompilerParams(vmem_limit_bytes=limit << 20),
        cost_estimate=cost,
        name=name,
    )
    settings.update(more)

    def space(place):
        if after is not None and place >= after:
            return pl.ANY
        return pltpu.SMEM if placed and place == 0 else pltpu.VMEM

    return lambda *arrays: pl.pallas_call(
        body,
        in_specs=[pl.BlockSpec(memory_space=space(place)) for place in range(len(arrays))],
        **settings,
    )(*arrays)


def on_device(behaviors, log_decay, qkv_weight, cotangent):
    rows = behaviors[0]
    rates = log_decay[0]
    upstream = cotangent[0]
    length, width = rows.shape
    heads = rates.shape[0]
    size = width // heads
    users = lax.axis_size("batch")
    count = lax.axis_size("seq")
    segments = count // heads
    chips = users // CORES
    pairs = heads // PAIR
    wide = PAIR * size
    at = jnp.stack([lax.axis_index("batch"), lax.axis_index("seq")]).astype(jnp.int32)

    def along_line(array, step):
        pairs_of = [(s, s // heads * heads + (s + step) % heads) for s in range(count)]
        return lax.ppermute(array, "seq", pairs_of)

    def along_segments(array, step):
        return lax.ppermute(array, "seq", [(s, (s + step * heads) % count) for s in range(count)])

    def along_users(array, step, turn):
        pairs_of = [
            (u, (u // CORES + step) % chips * CORES + (u + turn) % CORES) for u in range(users)
        ]
        return lax.ppermute(array, "batch", pairs_of)

    def line_exchange(arrays):
        order = sorted(range(1, heads), key=lambda step: -min(step, heads - step))
        return [arrays[0]] + [along_line(arrays[step], step) for step in order]

    whole = lambda dims: pl.BlockSpec(dims, lambda i: (0,) * len(dims))
    column = pl.BlockSpec((length, wide), lambda i: (0, i))
    weight_at = lambda part: pl.BlockSpec((width, wide), lambda i: (0, part * pairs + i))
    tokens = lambda kind: shape((length, width), kind)
    state = shape((size, size))
    smem = pl.BlockSpec(memory_space=pltpu.SMEM)
    share = heads * size // count
    slices = shape((count, share, size))
    square = length * length * size

    def exchange(own, other, moved):
        dims = own.shape[1:]
        came = along_users(other, 0, 1)
        both = kernel(
            pair_kernel, [shape((CORES,) + dims)] * chips, 1 << 16, moved, "pair", False
        )(own, came)
        return [both[0]] + [along_users(both[step], step, 0) for step in range(1, chips)]

    q, k, v, tall, flat, sums, top, low, weight_columns = pl.pallas_call(
        functools.partial(project_kernel, size),
        grid=(pairs,),
        in_specs=[smem, whole((length, width)), weight_at(0), weight_at(1), weight_at(2), whole((heads, length))],
        out_specs=[column] * 3 + [whole((length, heads)), whole((heads, length))]
        + [pl.BlockSpec((count // pairs, share + EXTRA, size), lambda i: (i, 0, 0))]
        + [whole((length // 2, width))] * 2 + [whole((width, 3 * size))],
        out_shape=[tokens(half)] * 3 + [shape((length, heads)), shape((heads, length))]
        + [shape((count, share + EXTRA, size))] + [shape((length // 2, width))] * 2
        + [shape((width, 3 * size), half)],
        scratch_shapes=[pltpu.VMEM((length, heads), flt)],
        compiler_params=pltpu.CompilerParams(vmem_limit_bytes=59 << 20),
        cost_estimate=pl.CostEstimate(
            flops=6 * length * width * width, bytes_accessed=8 * width * width, transcendentals=0
        ),
        name="project",
    )(at, rows, qkv_weight, qkv_weight, qkv_weight, rates)
    ahead, astern = (lambda array: along_users(array, 1, 0)), (lambda array: along_users(array, chips - 1, 0))
    top_before, low_behind = ahead(top), astern(low)
    low_before, top_behind = ahead(low), astern(top)
    top_beyond, low_beyond = ahead(top_before), astern(low_behind)
    near_wide = [top, low, top_before, low_before, top_beyond, low_beyond, top_behind, low_behind]
    far_wide = [along_users(array, 0, 1) for array in near_wide]

    def mark_of(*arrays):
        return sum(array[-EXTRA:, :size] for array in arrays)

    got = lax.all_to_all(sums, "seq", 0, 0)
    entered, block_rates = kernel(
        scan_kernel, [slices, shape((count, EXTRA, size))], 1 << 18, 1 << 20, "scan", False
    )(got, mark_of(top_before, low_behind))
    state_in = lax.all_to_all(entered, "seq", 0, 0).reshape(heads, size, size)

    weights, intra = kernel(
        functools.partial(weights_kernel, heads, size),
        [shape((heads, length, length), half), tokens(flt)],
        heads * 4 * square, 5 << 20, "weights", False,
    )(q, k, v, tall, flat)

    mixed, d_output, sums = kernel(
        functools.partial(mix_kernel, size),
        [tokens(half), tokens(half), slices],
        heads * 2 * square, 5 << 20, "mix", False,
    )(q, intra, upstream, tall, state_in, mark_of(low_before, top_behind))
    got = lax.all_to_all(sums, "seq", 0, 0)
    packed = kernel(
        functools.partial(pack_kernel, size),
        [shape((chips, length + size + EXTRA, size))] * CORES, 1 << 18, 3 << 20, "pack",
    )(at, d_output, state_in, rates)
    every = exchange(*packed, 3 << 20)

    def recall(wide, after, name):
        count = len(wide) // 2
        return kernel(
            recall_kernel,
            [shape((count, length, width), half), shape((count, length, 3 * size), half), shape((EXTRA, size))],
            6 * length * width * size * count, 8 << 20, name, False, after=2, limit=58,
            scratch_shapes=[pltpu.VMEM((count, length, width), flt), pltpu.SemaphoreType.DMA((2 * count,))],
        )(weight_columns, after, *wide)

    pieces = {(step, 0): near_wide[2 * step : 2 * step + 2] for step in range(chips)}
    pieces.update({(step, 1): far_wide[2 * step : 2 * step + 2] for step in range(chips)})
    wides = [piece for place in ORDER for piece in pieces[place]]
    first_rows, first_qkv, mark = recall(wides[: 2 * FIRST], mark_of(top_before), "recall")

    entered, mark = kernel(
        back_scan_kernel, [slices, shape((EXTRA, size))], 1 << 18, 1 << 20, "back_scan", False
    )(got, block_rates, mark + mark_of(top_beyond, low_beyond))
    back = lax.all_to_all(entered, "seq", 0, 0).reshape(heads, size, size)
    d_query, key_part, value_part = kernel(
        functools.partial(inner_kernel, size),
        [tokens(half), tokens(flt), tokens(flt)], heads * 10 * square, 6 << 20, "inner", False,
    )(q, k, v, d_output, weights, state_in, tall, flat)
    rest_rows, rest_qkv, mark = recall(wides[2 * FIRST :], mark, "recall_rest")
    *chosen, back_bf = kernel(
        choose_kernel, [shape((chips, size, size))] * CORES + [shape((heads, size, size), half)],
        1 << 18, 1 << 20, "choose",
    )(at, back, mark)
    owned = exchange(*chosen, 1 << 20)

    owner_tall, turned_query, key_inner, value_inner = kernel(
        functools.partial(owner_kernel, size),
        [shape((length, users)), shape((size, users * length), half)] + [shape((users, length, size))] * 2,
        users * 12 * square, 6 << 20, "owner", False,
        scratch_shapes=[pltpu.VMEM((users, length), flt), pltpu.VMEM((users, length + size, size), flt)],
    )(first_qkv, rest_qkv, *every)
    turned = kernel(
        functools.partial(late_kernel, size),
        shape((3 * size, users * length), half), users * 2 * square, 4 << 20, "late", False,
        scratch_shapes=[pltpu.VMEM((users, size, size), half)],
    )(first_qkv, rest_qkv, key_inner, value_inner, owner_tall, turned_query, *owned)

    weight_rows = lambda part: pl.BlockSpec((wide, width), lambda i: (i, part))
    d_rows = pl.pallas_call(
        functools.partial(rows_kernel, size),
        grid=(pairs,),
        in_specs=[whole((length, width))] * 5
        + [whole((heads, size, size)), whole((length, heads))]
        + [weight_rows(part) for part in range(3)],
        out_specs=column,
        out_shape=tokens(half),
        scratch_shapes=[pltpu.VMEM((length, width), half)] * 2,
        compiler_params=pltpu.CompilerParams(vmem_limit_bytes=24 << 20),
        cost_estimate=pl.CostEstimate(
            flops=6 * length * width * width, bytes_accessed=8 * width * width, transcendentals=0
        ),
        name="rows",
    )(d_query, key_part, value_part, k, v, back_bf, tall, qkv_weight, qkv_weight, qkv_weight)
    def term(step):
        return kernel(
            functools.partial(term_kernel, step),
            shape((3 * size, width // segments)),
            6 * users * length * size * width // segments, 3 << 20, "term",
        )(at, turned, first_rows, rest_rows)

    got = [along_segments(term(step), step) for step in (2, 1, 3)] + [term(0)]
    pieces = kernel(
        fold_kernel, [shape((width // count, 3 * size))] * heads, 1 << 20, 2 << 20, "fold",
        scratch_shapes=[pltpu.VMEM((heads, width // count, 3 * size), flt)], after=5,
    )(at, *got, d_rows)
    got = line_exchange(pieces)
    mine = kernel(gather_kernel, shape((width // count, 3 * size)), 1 << 18, 1 << 18, "gather", False)(*got)

    other = along_users(mine, 0, 1)
    both = kernel(both_kernel, shape((CORES, width // count, 3 * size)), 1 << 16, 1 << 17, "both", False)(mine, other)
    summed = [both] + [along_users(both, step, 0) for step in range(1, chips)]
    squares = kernel(square_kernel, shape((count, EXTRA, size)), 1 << 18, 1 << 18, "square", False)(*summed)
    squares = lax.all_to_all(squares, "seq", 0, 0)
    weight_step = kernel(
        step_kernel, shape((width // count, 3 * width)), 1 << 18, 1 << 20, "step",
        scratch_shapes=[pltpu.VMEM((heads, width // count, 3 * size), flt)],
    )(at, squares, *summed)

    return (mixed[None], d_rows[None], weight_step)


def solution(mesh):
    placed = (P("batch", "seq", None), P("batch", None, "seq"), P(), P("batch", "seq", None))
    return jax.shard_map(
        on_device,
        mesh=mesh,
        in_specs=placed,
        out_specs=(P("batch", "seq", None), P("batch", "seq", None), P("seq", None)),
        check_vma=False,
    )
```
